256 devices in a mesh: row: 8 (over x_lo, y), col: 32 (over z, x_hi, core).
Axes of the slice: x: 4 (x_hi: 2, x_lo: 2; x = x_hi * 2 + x_lo), y: 4, z: 8, core: 2. Of those that a mesh axis runs over, the one named last changes fastest.
Arguments:
- tokens: bfloat16 [512, 16384], P('col', 'row'), may hold values from -6 to 6
- weight: bfloat16 [16384, 32768], P('row', 'col'), may hold values from -0.21875 to 0.21875
- logits: float32 [3, 32768], P(None, 'col'), may hold values from -6 to 303
- cotangent: bfloat16 [512, 32768], P('row', 'col'), may hold values from -6 to 6
Outputs:
- mixed_out: bfloat16 [512, 32768], P('row', 'col')
- input_grad: bfloat16 [512, 16384], P('col', 'row')
- weight_grad: bfloat16 [16384, 32768], P('row', 'col')
- logit_grad: float32 [3, 32768], P(None, 'col')
The draws below stay inside these ranges and needn't reach their ends.
All inputs are finite; a program needn't handle non-finite values.
Results may differ from the reference program's by a relative error of at most 0.0049.
Values may be sent and summed in bfloat16 or wider, within the bound.
A program may use at most 64 MiB of HBM per device.

```python
import math
import jax
import jax.numpy as jnp
from jax import lax

D = 16384
FF = 32768
TOKENS = 512


def draw_weight(key, part):
    first, second, third = jax.random.split(key, 3)
    base = jnp.clip(jax.random.normal(first, (D, FF), jnp.float32), -4.0, 4.0)
    upper = 10.0
    row_scale = jnp.exp(jax.random.uniform(second, (D, 1), jnp.float32) * jnp.log(upper))
    col_scale = jnp.exp(jax.random.uniform(third, (1, FF), jnp.float32) * jnp.log(upper))
    return (base * row_scale * col_scale / (16.0 * jnp.sqrt(float(D)))).astype(jnp.bfloat16)


def draw_logits(key, part):
    first = jax.random.fold_in(key, 0)
    return jnp.clip(1.5 * jax.random.normal(first, (3, FF), jnp.float32), -6.0, 6.0)


def raised(result, own_key, source, target, shards_of, factor):
    owner, partner = [(jnp.arange(result.shape[position]) // (result.shape[position] // shards_of)).reshape([-1 if axis == position else 1 for axis in range(result.ndim)]) for position in (source, target)]
    chosen = jax.random.permutation(own_key, shards_of)[partner]
    strong = (owner == chosen) | (owner == (partner + shards_of // 2) % shards_of)
    return jnp.where(strong, factor * result, result)


def level_of(key, dims, shards, smallest, high):
    def one(dim, parts):
        heights = jax.random.uniform(jax.random.fold_in(jax.random.fold_in(key, 6), dim), (parts,), jnp.float32, smallest / len(shards), high / len(shards))
        return jnp.repeat(jnp.exp(heights), dims[dim] // parts).reshape((-1,) + (1,) * (len(dims) - dim - 1))

    level = one(*shards[0])
    for cut in shards[1:]:
        level = level * one(*cut)
    return level


def heavy_noise(own_key, dims, scale, reach, cuts, heavy, kind=jnp.bfloat16):
    result = scale * jax.random.normal(own_key, dims, jnp.float32)
    if cuts:
        result = result * level_of(own_key, dims, cuts, -0.22, 0.18)
    return jnp.clip(raised(result, jax.random.fold_in(own_key, 3), *heavy), -reach, reach).astype(kind)


def setup_inputs(seed: int = 0) -> dict:
    seeds = jax.random.split(jax.random.key(seed), 5)
    return {
        "tokens": heavy_noise(seeds[0], (TOKENS, D), 1.0, 6.0, ((0, 32), (1, 8)), (1, 0, 32, 2.75)),
        "weight": draw_weight(jax.random.fold_in(seeds[4], 71), 0),
        "logits": draw_logits(jax.random.fold_in(seeds[4], 71), 0),
        "cotangent": heavy_noise(seeds[3], (TOKENS, FF), 1.0, 6.0, ((0, 8), (1, 32)), (1, 0, 32, 2.75)),
    }


EPSILON = 1e-6
TWO_PI = 2.0 * math.pi
grid_levels = (1.0, 7.0, 127.0)


def quantize(master, peak, scores):
    shares = jax.nn.softmax(scores, axis=0)
    blended = jnp.zeros_like(master)
    slopes = jnp.zeros_like(master)
    candidates = []
    for number, level_value in enumerate(grid_levels):
        spacing = (peak + EPSILON) / level_value
        scaled = master / spacing
        angle_value = TWO_PI * scaled
        candidate = spacing * (scaled - jnp.sin(angle_value) / TWO_PI)
        blended = blended + shares[number] * candidate
        slopes = slopes + shares[number] * (1.0 - jnp.cos(angle_value))
        candidates.append(candidate)
    return shares, blended, slopes, candidates


def logit_slopes(shares, terms):
    return shares * (terms - jnp.sum(shares * terms, axis=0, keepdims=True))


def reference(tokens, weight, logits, cotangent):
    block_width = math.gcd(FF, 1024)
    block_count = FF // block_width

    def advance(running, index_value):
        offset = (index_value * block_width).astype(jnp.int32)
        master = lax.dynamic_slice_in_dim(weight, offset, block_width, 1).astype(jnp.float32)
        scores = lax.dynamic_slice_in_dim(logits, offset, block_width, 1)
        cot_block = lax.dynamic_slice_in_dim(cotangent, offset, block_width, 1)
        peak = jnp.max(jnp.abs(master), axis=0)
        shares, blended, slopes, candidates = quantize(master, peak, scores)
        blend_half = blended.astype(jnp.bfloat16)
        output_block = jnp.dot(tokens, blend_half, preferred_element_type=jnp.float32).astype(jnp.bfloat16)
        running = running + jnp.dot(cot_block, blend_half.T, preferred_element_type=jnp.float32)
        mixed_grad = jnp.dot(tokens.T, cot_block, preferred_element_type=jnp.float32)
        grad_block = (mixed_grad * slopes).astype(jnp.bfloat16)
        terms = jnp.stack([jnp.sum(mixed_grad * candidate, axis=0) for candidate in candidates])
        return running, (output_block, grad_block, logit_slopes(shares, terms))

    start_value = jnp.zeros((TOKENS, D), jnp.float32)
    summed, stacked = lax.scan(advance, start_value, jnp.arange(block_count, dtype=jnp.int32))
    output_blocks, grad_blocks, logit_blocks = stacked
    mixed_out = output_blocks.transpose(1, 0, 2).reshape(TOKENS, FF)
    weight_grad = grad_blocks.transpose(1, 0, 2).reshape(D, FF)
    logit_grad = logit_blocks.transpose(1, 0, 2).reshape(3, FF)
    return mixed_out, summed.astype(jnp.bfloat16), weight_grad, logit_grad
```

```python
import functools

import jax
import jax.numpy as jnp
from jax import lax
from jax.experimental import pallas as pl
from jax.experimental.pallas import tpu as pltpu
from jax.sharding import PartitionSpec as P

EPSILON = 1e-06
LEVELS = (1.0, 7.0, 127.0)
PI = 3.141592653589793
MESH = pl.DeviceIdType.MESH
F32, BF16 = jnp.float32, jnp.bfloat16

SIN_FINE = (
    3.1415927410125732, -5.167709827423096, 2.550069808959961, -0.5982421040534973, 0.07756038755178452,
)
COS_FINE = (
    0.9999999403953552, -4.934792995452881, 4.058412075042725, -1.3318802118301392, 0.2196968048810959,
)
SIN_WIDE = (3.141589641571045, -5.167367935180664, 2.543604850769043, -0.55839604139328)


def monic(coefficients):
    lead = coefficients[-1]
    return lead, tuple(c / lead for c in coefficients[:-1])


SIN0_LEAD, SIN0 = monic(SIN_FINE)
COS0_LEAD, COS0 = monic(COS_FINE)
SIN2_LEAD, SIN2 = monic(SIN_WIDE)
COS2_LEAD, COS2 = monic(COS_FINE)
Q = SIN0_LEAD * SIN0_LEAD
SIN1_LEAD, SIN1 = monic((7.0, -56.0 * Q, 112.0 * Q**2, -64.0 * Q**3))
COS1_LEAD, COS1 = monic((1.0, -24.0 * Q, 80.0 * Q**2, -64.0 * Q**3))
SIN_SCALE = (SIN0_LEAD, SIN0_LEAD * SIN1_LEAD, SIN2_LEAD)
COS_SCALE = (COS0_LEAD, COS0_LEAD * COS1_LEAD, COS2_LEAD)


def horner(coefficients, x):
    total = x + coefficients[-1]
    for c in coefficients[-2::-1]:
        total = total * x + c
    return total


def soft_round(w, inv0, inv2, blend, slope):
    u0 = w * inv0
    r0 = u0 - jnp.round(u0)
    t0 = r0 * r0
    s0 = r0 * horner(SIN0, t0)
    c0 = horner(COS0, t0)
    z0 = s0 * s0
    p0 = s0 * c0
    s1 = s0 * horner(SIN1, z0)
    c1 = c0 * horner(COS1, z0)
    p1 = s1 * c1
    u2 = w * inv2
    r2 = u2 - jnp.round(u2)
    t2 = r2 * r2
    s2 = r2 * horner(SIN2, t2)
    c2 = horner(COS2, t2)
    p2 = s2 * c2
    blended = w - (blend[0] * p0 + blend[1] * p1 + blend[2] * p2)
    slopes = slope[0] * z0 + slope[1] * (s1 * s1) + slope[2] * (s2 * s2)
    return blended, slopes, p0, p1, p2


def body(
    R, Z, chunks, tile,
    tok_in, w_in, logits, cot_in,
    mixed_out, input_out, wg_out, lg_out,
    wv, slo, pr0, pr1, pr2, tokb, cotb, coef, pkb, trb, sums,
    igs, igr, own, rs_r, rs_l, rr_r, rr_l, xs, xr, ots, otr,
    w_sem, loc_sem, wo_sem, row_send, row_recv, tok_send, tok_recv, ring_send, ring_recv,
    ig_send, ig_recv,
):
    D, F = wv.shape
    H = Z // 2
    r = lax.axis_index("row")
    col = lax.axis_index("col")
    z, xh, c = col // 4, (col // 2) % 2, col % 2
    right = (r, ((z + 1) % Z) * 4 + xh * 2 + c)
    left = (r, ((z + Z - 1) % Z) * 4 + xh * 2 + c)
    across = (r, z * 4 + (1 - xh) * 2 + c)
    sibling = (r, z * 4 + xh * 2 + (1 - c))
    sent = []

    def send(src, dst, ssem, rsem, to):
        copy = pltpu.make_async_remote_copy(
            src_ref=src, dst_ref=dst, send_sem=ssem, recv_sem=rsem, device_id=to, device_id_type=MESH
        )
        copy.start()
        sent.append(copy)
        return copy

    def plane(which):
        return (which + 2 * Z) % Z

    barrier = pltpu.get_barrier_semaphore()
    partners = [((r + k) % R, col) for k in range(1, R)] + [right, left, across, sibling]
    for to in partners:
        pl.semaphore_signal(barrier, inc=1, device_id=to, device_id_type=MESH)
    n_w = w_sem.shape[0]
    w_rows = D // n_w
    w_copies = []
    own_tok = pltpu.make_async_copy(tok_in, tokb.at[c, z, pl.ds(xh * 16, 16)], loc_sem.at[0])
    own_tok.start()
    own_cot = []
    for a in range(2):
        for b in range(2):
            copy = pltpu.make_async_copy(
                cot_in.at[pl.ds((a * 2 + b) * 16, 16)], cotb.at[b, r, pl.ds(a * 16, 16)], loc_sem.at[1 + a * 2 + b]
            )
            copy.start()
            own_cot.append(copy)
    for k in range(n_w):
        rows = pl.ds(k * w_rows, w_rows)
        copy = pltpu.make_async_copy(w_in.at[rows], wv.at[rows], w_sem.at[k])
        copy.start()
        w_copies.append(copy)
    pl.semaphore_wait(barrier, len(partners))

    own_tok.wait()
    mine = tokb.at[c, z, pl.ds(xh * 16, 16)]
    tok_x = send(mine, mine, tok_send.at[0], tok_recv.at[0], across)
    for copy in own_cot:
        copy.wait()
    cots = [
        send(cotb.at[:, r], cotb.at[:, r], row_send.at[0, k], row_recv.at[0, k], ((r + k) % R, col))
        for k in range(1, R)
    ]

    best = jnp.zeros((16, F), BF16)
    for k in range(n_w):
        w_copies[k].wait()

        def step(i, best, k=k):
            rows = pl.ds(pl.multiple_of(k * w_rows + i * 16, 16), 16)
            return jnp.maximum(best, jnp.abs(wv[rows, :]))

        best = lax.fori_loop(0, w_rows // 16, step, best)
    local = jnp.max(best.astype(F32), axis=0, keepdims=True)
    lanes = F // 128
    for i in range(lanes):
        pkb[r, i : i + 1, :] = local[:, i * 128 : (i + 1) * 128]
    peaks = [
        send(pkb.at[r], pkb.at[r], row_send.at[1, k], row_recv.at[1, k], ((r + k) % R, col)) for k in range(1, R)
    ]

    tok_x.wait_recv()
    piece = tokb.at[c, z]
    sib0 = send(piece, piece, tok_send.at[1], tok_recv.at[1], sibling)
    tok_r = [send(piece, piece, ring_send.at[0, 0], ring_recv.at[0, 0], right)]
    tok_l = [send(piece, piece, ring_send.at[1, 0], ring_recv.at[1, 0], left)]
    sibs = [sib0]

    def tok_step(k):
        tok_r[k].wait_recv()
        tok_l[k].wait_recv()
        half = k == H - 1
        from_left, from_right = plane(z - k - 1), plane(z + k + 1)
        if not half:
            a, b = tokb.at[c, from_left], tokb.at[c, from_right]
            if k == H - 2:
                fa, fb = tokb.at[c, from_left, pl.ds(0, 16)], tokb.at[c, from_right, pl.ds(16, 16)]
            else:
                fa, fb = a, b
            tok_r.append(send(fa, fa, ring_send.at[0, k + 1], ring_recv.at[0, k + 1], right))
            tok_l.append(send(fb, fb, ring_send.at[1, k + 1], ring_recv.at[1, k + 1], left))
            sibs.append(send(a, a, tok_send.at[2 + 2 * k], tok_recv.at[2 + 2 * k], sibling))
            sibs.append(send(b, b, tok_send.at[3 + 2 * k], tok_recv.at[3 + 2 * k], sibling))
        else:
            a = tokb.at[c, from_left]
            sibs.append(send(a, a, tok_send.at[2 + 2 * k], tok_recv.at[2 + 2 * k], sibling))

    scores = logits[...]
    top = jnp.max(scores, axis=0, keepdims=True)
    raised = jnp.exp(scores - top)
    shares = raised / jnp.sum(raised, axis=0, keepdims=True)
    for copy in peaks:
        copy.wait_recv()
    peak8 = pkb[0]
    for i in range(1, R):
        peak8 = jnp.maximum(peak8, pkb[i])
    for i in range(lanes):
        coef[0:1, i * 128 : (i + 1) * 128] = peak8[i : i + 1, :]
    padded = coef[0:1, :] + EPSILON
    coef[0:1, :] = LEVELS[0] / padded
    coef[1:2, :] = LEVELS[2] / padded
    for b in range(3):
        share = shares[b : b + 1]
        factor = (padded / LEVELS[b]) * (SIN_SCALE[b] * COS_SCALE[b] / PI)
        coef[2 + b : 3 + b, :] = share * factor
        coef[5 + b : 6 + b, :] = share * (2.0 * SIN_SCALE[b] * SIN_SCALE[b])
        coef[8 + b : 9 + b, :] = factor
        coef[11 + b : 12 + b, :] = share

    rows_a = 64

    def blend_rows(first, last):
        for lane in range(lanes):
            cs = pl.ds(lane * 128, 128)
            k = [jnp.broadcast_to(coef[i : i + 1, cs], (rows_a, 128)) for i in range(8)]

            def step(i, carry, cs=cs, k=k):
                rs = pl.ds(pl.multiple_of(i * rows_a, rows_a), rows_a)
                w = wv[rs, cs].astype(F32)
                blended, slopes, p0, p1, p2 = soft_round(w, k[0], k[1], k[2:5], k[5:8])
                wv[rs, cs] = blended.astype(BF16)
                slo[rs, cs] = slopes
                pr0[rs, cs] = p0
                pr1[rs, cs] = p1
                pr2[rs, cs] = p2
                return carry

            lax.fori_loop(first // rows_a, last // rows_a, step, 0)

    width = D // chunks
    NT = (((1,), (1,)), ((), ()))
    chains = [dict() for _ in range(chunks)]

    def ig_dot(q):
        def step(i, carry):
            rs = pl.ds(pl.multiple_of(q * width + i * tile, tile), tile)
            blend = wv[rs, :]
            theirs = lax.dot_general(
                cotb[1 - c].reshape(Z * 32, F), blend, NT, preferred_element_type=F32
            )
            igs[:, :, rs] = theirs.astype(BF16).reshape(Z, 32, tile)
            ours = lax.dot_general(cotb[c].reshape(Z * 32, F), blend, NT, preferred_element_type=F32)
            own[:, :, rs] = ours.reshape(Z, 32, tile)
            return carry

        lax.fori_loop(0, width // tile, step, 0)
        cs = pl.ds(q * width, width)
        chains[q]["core"] = send(
            igs.at[:, :, cs], igr.at[:, :, cs], ig_send.at[q, 0], ig_recv.at[q, 0], sibling
        )

    def ig_hop(q, k):
        cs = pl.ds(q * width, width)
        chain = chains[q]
        if k == 0:
            chain["core"].wait_recv()
        else:
            chain["r"].wait_recv()
            chain["l"].wait_recv()

        def term(which, first, count):
            rows = pl.ds(first, count)
            return own[which, rows, cs] + igr[which, rows, cs].astype(F32)

        if k == 0:
            rs_r[0, 0:16, cs] = term(plane(z + H), 0, 16).astype(BF16)
            rs_l[0, 0:16, cs] = term(plane(z + H), 16, 16).astype(BF16)
        elif k == 1 and H > 1:
            for buf, got, to, a in ((rs_r, rr_r, z + H - 1, 0), (rs_l, rr_l, z - H + 1, 16)):
                buf[1, pl.ds(a, 16), cs] = (
                    term(plane(to), a, 16) + got[0, 0:16, cs].astype(F32)
                ).astype(BF16)
                buf[1, pl.ds(16 - a, 16), cs] = term(plane(to), 16 - a, 16).astype(BF16)
        elif k < H:
            for buf, got, to in ((rs_r, rr_r, z + H - k), (rs_l, rr_l, z - H + k)):
                buf[k, :, cs] = (term(plane(to), 0, 32) + got[k - 1, :, cs].astype(F32)).astype(BF16)
        if k < H:
            rows = pl.ds(0, 16 if k == 0 else 32)
            for name, buf, got, to, d in (("r", rs_r, rr_r, right, 0), ("l", rs_l, rr_l, left, 1)):
                chain[name] = send(
                    buf.at[k, rows, cs], got.at[k, rows, cs],
                    ig_send.at[q, 1 + 2 * k + d], ig_recv.at[q, 1 + 2 * k + d], to,
                )
        else:
            for p in range(2):
                rows = pl.ds(p * 16, 16)
                total = term(z, p * 16, 16)
                if H > 1:
                    total = total + (rr_r[H - 1, rows, cs].astype(F32) + rr_l[H - 1, rows, cs].astype(F32))
                else:
                    total = total + (rr_r, rr_l)[p][0, 0:16, cs].astype(F32)
                own[z, rows, cs] = total
                xs[p, :, cs] = total.astype(BF16)
            chain["x"] = send(
                xs.at[1 - xh, :, cs], xr.at[:, cs], ig_send.at[q, 1 + 2 * H], ig_recv.at[q, 1 + 2 * H], across
            )

    def ig_end(q):
        cs = pl.ds(q * width, width)
        chains[q]["x"].wait_recv()
        total = own[z, pl.ds(pl.multiple_of(xh * 16, 16), 16), cs] + xr[:, cs].astype(F32)
        input_out[:, cs] = total.astype(BF16)

    def out_dot():
        def step(i, carry):
            cs = pl.ds(pl.multiple_of(i * tile, tile), tile)
            part = jnp.dot(
                tokb[...].reshape(2 * Z * 32, D), wv[:, cs], preferred_element_type=F32
            ).astype(BF16)
            part = part.reshape(2, Z, 32, tile)
            for a in range(2):
                ots[:, pl.ds(a * 32, 32), cs] = part[a]
            return carry

        lax.fori_loop(0, F // tile, step, 0)
        return [
            send(ots.at[(r + k) % R], otr.at[r], row_send.at[2, k], row_recv.at[2, k], ((r + k) % R, col))
            for k in range(1, R)
        ]

    def out_end(copies):
        for copy in copies:
            copy.wait_recv()
        otr[r] = ots[r]
        for a in range(2):
            for b in range(2):
                rows = pl.ds(a * 32 + b * 16, 16)
                total = otr[0, rows, :].astype(F32)
                for i in range(1, R):
                    total = total + otr[i, rows, :].astype(F32)
                mixed_out[pl.ds((b * 2 + a) * 16, 16), :] = total.astype(BF16)

    grads = []
    TN = (((0,), (0,)), ((), ()))

    def grad_rows(t):
        rs = pl.ds(t * tile, tile)
        flat = tokb[:, :, :, rs].reshape(2 * Z * 32, tile)

        def step(i, carry):
            cs = pl.ds(pl.multiple_of(i * tile, tile), tile)
            mg = lax.dot_general(
                flat, cotb[:, :, :, cs].reshape(2 * Z * 32, tile), TN, preferred_element_type=F32
            )
            wv[rs, cs] = (mg * slo[rs, cs]).astype(BF16)
            for b, pr in enumerate((pr0, pr1, pr2)):
                part = jnp.sum((mg * pr[rs, cs]).reshape(tile // 8, 8, tile), axis=0)
                sums[b, :, cs] = part if t == 0 else sums[b, :, cs] + part
            return carry

        lax.fori_loop(0, F // tile, step, 0)
        copy = pltpu.make_async_copy(wv.at[rs], wg_out.at[rs], wo_sem.at[t])
        copy.start()
        grads.append(copy)

    tiles = D // tile
    half = tiles // 2
    assert chunks == 2
    hops = [functools.partial(tok_step, k) for k in range(H)]
    for t in range(half):
        blend_rows(t * tile, (t + 1) * tile)
        if hops:
            hops.pop(0)()
    for copy in cots:
        copy.wait_recv()
    ig_dot(0)
    first = [functools.partial(ig_hop, 0, k) for k in range(H + 1)] + [functools.partial(ig_end, 0)]
    for t in range(half, tiles):
        blend_rows(t * tile, (t + 1) * tile)
        if hops:
            hops.pop(0)()
        first.pop(0)()
    while hops:
        hops.pop(0)()
    ig_dot(1)
    for copy in sibs:
        copy.wait_recv()
    outs = out_dot()
    second = [functools.partial(ig_hop, 1, k) for k in range(H + 1)] + [functools.partial(ig_end, 1)]
    for t in range(tiles):
        if first:
            first.pop(0)()
        second.pop(0)() if second else None
        grad_rows(t)
    for pending in (first, second):
        while pending:
            pending.pop(0)()
    for b in range(3):
        total = jnp.sum(sums[b], axis=0, keepdims=True)
        for i in range(lanes):
            trb[r, b, i : i + 1, :] = total[:, i * 128 : (i + 1) * 128]
    terms = [
        send(trb.at[r], trb.at[r], row_send.at[3, k], row_recv.at[3, k], ((r + k) % R, col)) for k in range(1, R)
    ]
    out_end(outs)
    for copy in terms:
        copy.wait_recv()
    total = trb[0]
    for i in range(1, R):
        total = total + trb[i]
    for i in range(lanes):
        cs = pl.ds(i * 128, 128)
        scaled = [coef[8 + b : 9 + b, cs] * total[b, i : i + 1, :] for b in range(3)]
        share = [coef[11 + b : 12 + b, cs] for b in range(3)]
        mean = share[0] * scaled[0] + share[1] * scaled[1] + share[2] * scaled[2]
        for b in range(3):
            lg_out[b : b + 1, cs] = share[b] * (mean - scaled[b])
    for copy in sent:
        copy.wait_send()
    for copy in grads:
        copy.wait()


def shards(R, Z, tokens, weight, logits, cotangent):
    D, F = weight.shape
    H = Z // 2
    chunks, tile = 2, min(256, D // 8)
    T = 2 * Z * 32
    rows = cotangent.shape[0]
    n_w = 4
    vmem = pltpu.VMEM
    dma = pltpu.SemaphoreType.DMA
    scratch = [
        vmem((D, F), BF16), vmem((D, F), F32), vmem((D, F), F32), vmem((D, F), F32), vmem((D, F), F32),
        vmem((2, Z, 32, D), BF16), vmem((2, R, 32, F), BF16), vmem((16, F), F32),
        vmem((R, F // 128, 128), F32), vmem((R, 3, F // 128, 128), F32), vmem((3, 8, F), F32),
        vmem((Z, 32, D), BF16), vmem((Z, 32, D), BF16), vmem((Z, 32, D), F32),
        vmem((H, 32, D), BF16), vmem((H, 32, D), BF16), vmem((H, 32, D), BF16), vmem((H, 32, D), BF16),
        vmem((2, 16, D), BF16), vmem((16, D), BF16),
        vmem((R, rows, F), BF16), vmem((R, rows, F), BF16),
        dma((n_w,)), dma((5,)), dma((D // tile,)), dma((4, R)), dma((4, R)),
        dma((2 + 2 * H,)), dma((2 + 2 * H,)), dma((2, H)), dma((2, H)),
        dma((chunks, 2 + 2 * H)), dma((chunks, 2 + 2 * H)),
    ]
    return pl.pallas_call(
        functools.partial(body, R, Z, chunks, tile),
        out_shape=(
            jax.ShapeDtypeStruct((rows, F), BF16),
            jax.ShapeDtypeStruct((16, D), BF16),
            jax.ShapeDtypeStruct((D, F), BF16),
            jax.ShapeDtypeStruct((3, F), F32),
        ),
        in_specs=[
            pl.BlockSpec(memory_space=pl.ANY), pl.BlockSpec(memory_space=pl.ANY),
            pl.BlockSpec(memory_space=vmem), pl.BlockSpec(memory_space=pl.ANY),
        ],
        out_specs=(
            pl.BlockSpec(memory_space=vmem), pl.BlockSpec(memory_space=vmem),
            pl.BlockSpec(memory_space=pl.ANY), pl.BlockSpec(memory_space=vmem),
        ),
        scratch_shapes=scratch,
        compiler_params=pltpu.CompilerParams(
            collective_id=0, has_side_effects=True, vmem_limit_bytes=58 * 2**20
        ),
    )(tokens, weight, logits, cotangent)


def solution(mesh):
    R, Z = mesh.shape["row"], mesh.shape["col"] // 4
    in_specs = (P("col", "row"), P("row", "col"), P(None, "col"), P("row", "col"))
    out_specs = (P("row", "col"), P("col", "row"), P("row", "col"), P(None, "col"))
    return jax.shard_map(
        functools.partial(shards, R, Z), mesh=mesh, in_specs=in_specs, out_specs=out_specs, check_vma=False
    )
```

```python
import functools

import jax
import jax.numpy as jnp
from jax import lax
from jax.experimental import pallas as pl
from jax.experimental.pallas import tpu as pltpu
from jax.sharding import PartitionSpec as P

EPSILON = 1e-06
LEVELS = (1.0, 7.0, 127.0)
PI = 3.141592653589793
MESH = pl.DeviceIdType.MESH
F32, BF16 = jnp.float32, jnp.bfloat16

SIN_FINE = (
    3.1415927410125732, -5.167709827423096, 2.550069808959961, -0.5982421040534973, 0.07756038755178452,
)
COS_FINE = (
    0.9999999403953552, -4.934792995452881, 4.058412075042725, -1.3318802118301392, 0.2196968048810959,
)
SIN_WIDE = (3.141589641571045, -5.167367935180664, 2.543604850769043, -0.55839604139328)


def monic(coefficients):
    lead = coefficients[-1]
    return lead, tuple(c / lead for c in coefficients[:-1])


SIN0_LEAD, SIN0 = monic(SIN_FINE)
COS0_LEAD, COS0 = monic(COS_FINE)
SIN2_LEAD, SIN2 = monic(SIN_WIDE)
COS2_LEAD, COS2 = monic(COS_FINE)
Q = SIN0_LEAD * SIN0_LEAD
SIN1_LEAD, SIN1 = monic((7.0, -56.0 * Q, 112.0 * Q**2, -64.0 * Q**3))
COS1_LEAD, COS1 = monic((1.0, -24.0 * Q, 80.0 * Q**2, -64.0 * Q**3))
SIN_SCALE = (SIN0_LEAD, SIN0_LEAD * SIN1_LEAD, SIN2_LEAD)
COS_SCALE = (COS0_LEAD, COS0_LEAD * COS1_LEAD, COS2_LEAD)


def horner(coefficients, x):
    total = x + coefficients[-1]
    for c in coefficients[-2::-1]:
        total = total * x + c
    return total


def soft_round(w, inv0, inv2, blend, slope):
    u0 = w * inv0
    r0 = u0 - jnp.round(u0)
    t0 = r0 * r0
    s0 = r0 * horner(SIN0, t0)
    c0 = horner(COS0, t0)
    z0 = s0 * s0
    p0 = s0 * c0
    s1 = s0 * horner(SIN1, z0)
    c1 = c0 * horner(COS1, z0)
    p1 = s1 * c1
    u2 = w * inv2
    r2 = u2 - jnp.round(u2)
    t2 = r2 * r2
    s2 = r2 * horner(SIN2, t2)
    c2 = horner(COS2, t2)
    p2 = s2 * c2
    blended = w - (blend[0] * p0 + blend[1] * p1 + blend[2] * p2)
    slopes = slope[0] * z0 + slope[1] * (s1 * s1) + slope[2] * (s2 * s2)
    return blended, slopes, p0, p1, p2


def body(
    R, Z, chunks, tile,
    tok_in, w_in, logits, cot_in,
    mixed_out, input_out, wg_out, lg_out,
    wv, slo, pr0, pr1, pr2, tokb, cotb, coef, pkb, trb, sums,
    igs, igr, own, rs_r, rs_l, rr_r, rr_l, xs, xr, ots, otr,
    w_sem, loc_sem, wo_sem, row_send, row_recv, tok_send, tok_recv, ring_send, ring_recv,
    ig_send, ig_recv,
):
    D, F = wv.shape
    H = Z // 2
    r = lax.axis_index("row")
    col = lax.axis_index("col")
    z, xh, c = col // 4, (col // 2) % 2, col % 2
    right = (r, ((z + 1) % Z) * 4 + xh * 2 + c)
    left = (r, ((z + Z - 1) % Z) * 4 + xh * 2 + c)
    across = (r, z * 4 + (1 - xh) * 2 + c)
    sibling = (r, z * 4 + xh * 2 + (1 - c))
    sent = []

    def send(src, dst, ssem, rsem, to):
        copy = pltpu.make_async_remote_copy(
            src_ref=src, dst_ref=dst, send_sem=ssem, recv_sem=rsem, device_id=to, device_id_type=MESH
        )
        copy.start()
        sent.append(copy)
        return copy

    def plane(which):
        return (which + 2 * Z) % Z

    barrier = pltpu.get_barrier_semaphore()
    partners = [((r + k) % R, col) for k in range(1, R)] + [right, left, across, sibling]
    for to in partners:
        pl.semaphore_signal(barrier, inc=1, device_id=to, device_id_type=MESH)
    n_w = w_sem.shape[0]
    w_rows = D // n_w
    w_copies = []
    own_tok = pltpu.make_async_copy(tok_in, tokb.at[c, z, pl.ds(xh * 16, 16)], loc_sem.at[0])
    own_tok.start()
    own_cot = []
    for a in range(2):
        for b in range(2):
            copy = pltpu.make_async_copy(
                cot_in.at[pl.ds((a * 2 + b) * 16, 16)], cotb.at[b, r, pl.ds(a * 16, 16)], loc_sem.at[1 + a * 2 + b]
            )
            copy.start()
            own_cot.append(copy)
    for k in range(n_w):
        rows = pl.ds(k * w_rows, w_rows)
        copy = pltpu.make_async_copy(w_in.at[rows], wv.at[rows], w_sem.at[k])
        copy.start()
        w_copies.append(copy)
    pl.semaphore_wait(barrier, len(partners))

    own_tok.wait()
    mine = tokb.at[c, z, pl.ds(xh * 16, 16)]
    tok_x = send(mine, mine, tok_send.at[0], tok_recv.at[0], across)

    best = jnp.zeros((16, F), BF16)
    for k in range(n_w):
        w_copies[k].wait()

        def step(i, best, k=k):
            rows = pl.ds(pl.multiple_of(k * w_rows + i * 16, 16), 16)
            return jnp.maximum(best, jnp.abs(wv[rows, :]))

        best = lax.fori_loop(0, w_rows // 16, step, best)
    local = jnp.max(best.astype(F32), axis=0, keepdims=True)
    lanes = F // 128
    for i in range(lanes):
        pkb[r, i : i + 1, :] = local[:, i * 128 : (i + 1) * 128]
    peaks = [
        send(pkb.at[r], pkb.at[r], row_send.at[1, k], row_recv.at[1, k], ((r + k) % R, col)) for k in range(1, R)
    ]

    for copy in own_cot:
        copy.wait()
    cots = [
        send(cotb.at[:, r], cotb.at[:, r], row_send.at[0, k], row_recv.at[0, k], ((r + k) % R, col))
        for k in range(1, R)
    ]
    tok_x.wait_recv()
    piece = tokb.at[c, z]
    sib0 = send(piece, piece, tok_send.at[1], tok_recv.at[1], sibling)
    tok_r = [send(piece, piece, ring_send.at[0, 0], ring_recv.at[0, 0], right)]
    tok_l = [send(piece, piece, ring_send.at[1, 0], ring_recv.at[1, 0], left)]
    sibs = [sib0]

    def tok_step(k):
        tok_r[k].wait_recv()
        tok_l[k].wait_recv()
        half = k == H - 1
        from_left, from_right = plane(z - k - 1), plane(z + k + 1)
        if not half:
            a, b = tokb.at[c, from_left], tokb.at[c, from_right]
            if k == H - 2:
                fa, fb = tokb.at[c, from_left, pl.ds(0, 16)], tokb.at[c, from_right, pl.ds(16, 16)]
            else:
                fa, fb = a, b
            tok_r.append(send(fa, fa, ring_send.at[0, k + 1], ring_recv.at[0, k + 1], right))
            tok_l.append(send(fb, fb, ring_send.at[1, k + 1], ring_recv.at[1, k + 1], left))
            sibs.append(send(a, a, tok_send.at[2 + 2 * k], tok_recv.at[2 + 2 * k], sibling))
            sibs.append(send(b, b, tok_send.at[3 + 2 * k], tok_recv.at[3 + 2 * k], sibling))
        else:
            a = tokb.at[c, from_left]
            sibs.append(send(a, a, tok_send.at[2 + 2 * k], tok_recv.at[2 + 2 * k], sibling))

    scores = logits[...]
    top = jnp.max(scores, axis=0, keepdims=True)
    raised = jnp.exp(scores - top)
    shares = raised / jnp.sum(raised, axis=0, keepdims=True)
    for copy in peaks:
        copy.wait_recv()
    peak8 = pkb[0]
    for i in range(1, R):
        peak8 = jnp.maximum(peak8, pkb[i])
    for i in range(lanes):
        coef[0:1, i * 128 : (i + 1) * 128] = peak8[i : i + 1, :]
    padded = coef[0:1, :] + EPSILON
    coef[0:1, :] = LEVELS[0] / padded
    coef[1:2, :] = LEVELS[2] / padded
    for b in range(3):
        share = shares[b : b + 1]
        factor = (padded / LEVELS[b]) * (SIN_SCALE[b] * COS_SCALE[b] / PI)
        coef[2 + b : 3 + b, :] = share * factor
        coef[5 + b : 6 + b, :] = share * (2.0 * SIN_SCALE[b] * SIN_SCALE[b])
        coef[8 + b : 9 + b, :] = factor
        coef[11 + b : 12 + b, :] = share

    rows_a = 64

    def blend_rows(first, last, some=None):
        for lane in some or range(lanes):
            cs = pl.ds(lane * 128, 128)
            k = [jnp.broadcast_to(coef[i : i + 1, cs], (rows_a, 128)) for i in range(8)]

            def step(i, carry, cs=cs, k=k):
                rs = pl.ds(pl.multiple_of(i * rows_a, rows_a), rows_a)
                w = wv[rs, cs].astype(F32)
                blended, slopes, p0, p1, p2 = soft_round(w, k[0], k[1], k[2:5], k[5:8])
                wv[rs, cs] = blended.astype(BF16)
                slo[rs, cs] = slopes
                pr0[rs, cs] = p0
                pr1[rs, cs] = p1
                pr2[rs, cs] = p2
                return carry

            lax.fori_loop(first // rows_a, last // rows_a, step, 0)

    width = D // chunks
    NT = (((1,), (1,)), ((), ()))
    chains = [dict() for _ in range(chunks)]

    def ig_dot(q):
        def step(i, carry):
            rs = pl.ds(pl.multiple_of(q * width + i * tile, tile), tile)
            blend = wv[rs, :]
            theirs = lax.dot_general(
                cotb[1 - c].reshape(Z * 32, F), blend, NT, preferred_element_type=F32
            )
            igs[:, :, rs] = theirs.astype(BF16).reshape(Z, 32, tile)
            ours = lax.dot_general(cotb[c].reshape(Z * 32, F), blend, NT, preferred_element_type=F32)
            own[:, :, rs] = ours.reshape(Z, 32, tile)
            return carry

        lax.fori_loop(0, width // tile, step, 0)
        cs = pl.ds(q * width, width)
        chains[q]["core"] = send(
            igs.at[:, :, cs], igr.at[:, :, cs], ig_send.at[q, 0], ig_recv.at[q, 0], sibling
        )

    def ig_hop(q, k):
        cs = pl.ds(q * width, width)
        chain = chains[q]
        if k == 0:
            chain["core"].wait_recv()
        else:
            chain["r"].wait_recv()
            chain["l"].wait_recv()

        def term(which, first, count):
            rows = pl.ds(first, count)
            return own[which, rows, cs] + igr[which, rows, cs].astype(F32)

        if k == 0:
            rs_r[0, 0:16, cs] = term(plane(z + H), 0, 16).astype(BF16)
            rs_l[0, 0:16, cs] = term(plane(z + H), 16, 16).astype(BF16)
        elif k == 1 and H > 1:
            for buf, got, to, a in ((rs_r, rr_r, z + H - 1, 0), (rs_l, rr_l, z - H + 1, 16)):
                buf[1, pl.ds(a, 16), cs] = (
                    term(plane(to), a, 16) + got[0, 0:16, cs].astype(F32)
                ).astype(BF16)
                buf[1, pl.ds(16 - a, 16), cs] = term(plane(to), 16 - a, 16).astype(BF16)
        elif k < H:
            for buf, got, to in ((rs_r, rr_r, z + H - k), (rs_l, rr_l, z - H + k)):
                buf[k, :, cs] = (term(plane(to), 0, 32) + got[k - 1, :, cs].astype(F32)).astype(BF16)
        if k < H:
            rows = pl.ds(0, 16 if k == 0 else 32)
            for name, buf, got, to, d in (("r", rs_r, rr_r, right, 0), ("l", rs_l, rr_l, left, 1)):
                chain[name] = send(
                    buf.at[k, rows, cs], got.at[k, rows, cs],
                    ig_send.at[q, 1 + 2 * k + d], ig_recv.at[q, 1 + 2 * k + d], to,
                )
        else:
            for p in range(2):
                rows = pl.ds(p * 16, 16)
                total = term(z, p * 16, 16)
                if H > 1:
                    total = total + (rr_r[H - 1, rows, cs].astype(F32) + rr_l[H - 1, rows, cs].astype(F32))
                else:
                    total = total + (rr_r, rr_l)[p][0, 0:16, cs].astype(F32)
                own[z, rows, cs] = total
                xs[p, :, cs] = total.astype(BF16)
            chain["x"] = send(
                xs.at[1 - xh, :, cs], xr.at[:, cs], ig_send.at[q, 1 + 2 * H], ig_recv.at[q, 1 + 2 * H], across
            )

    def ig_end(q):
        cs = pl.ds(q * width, width)
        chains[q]["x"].wait_recv()
        total = own[z, pl.ds(pl.multiple_of(xh * 16, 16), 16), cs] + xr[:, cs].astype(F32)
        input_out[:, cs] = total.astype(BF16)

    def out_dot(part_of, parts):
        span = F // parts

        def step(i, carry):
            cs = pl.ds(pl.multiple_of(part_of * span + i * tile, tile), tile)
            part = jnp.dot(
                tokb[...].reshape(2 * Z * 32, D), wv[:, cs], preferred_element_type=F32
            ).astype(BF16)
            part = part.reshape(2, Z, 32, tile)
            for a in range(2):
                ots[:, pl.ds(a * 32, 32), cs] = part[a]
            return carry

        lax.fori_loop(0, span // tile, step, 0)
        cs = pl.ds(part_of * span, span)
        return [
            send(
                ots.at[(r + k) % R, :, cs], otr.at[r, :, cs],
                row_send.at[2 + part_of, k], row_recv.at[2 + part_of, k], ((r + k) % R, col),
            )
            for k in range(1, R)
        ]

    def out_end(copies):
        for copy in copies:
            copy.wait_recv()
        otr[r] = ots[r]
        for a in range(2):
            for b in range(2):
                rows = pl.ds(a * 32 + b * 16, 16)
                total = otr[0, rows, :].astype(F32)
                for i in range(1, R):
                    total = total + otr[i, rows, :].astype(F32)
                mixed_out[pl.ds((b * 2 + a) * 16, 16), :] = total.astype(BF16)

    grads = []

    def grad_rows(t):
        rs = pl.ds(t * tile, tile)
        turned = tokb[:, :, :, rs].reshape(2 * Z * 32, tile).T

        def step(i, carry):
            cs = pl.ds(pl.multiple_of(i * tile, tile), tile)
            mg = jnp.dot(
                turned, cotb[:, :, :, cs].reshape(2 * Z * 32, tile), preferred_element_type=F32
            )
            wv[rs, cs] = (mg * slo[rs, cs]).astype(BF16)
            for b, pr in enumerate((pr0, pr1, pr2)):
                part = jnp.sum((mg * pr[rs, cs]).reshape(tile // 8, 8, tile), axis=0)
                sums[b, :, cs] = part if t == 0 else sums[b, :, cs] + part
            return carry

        lax.fori_loop(0, F // tile, step, 0)
        copy = pltpu.make_async_copy(wv.at[rs], wg_out.at[rs], wo_sem.at[t])
        copy.start()
        grads.append(copy)

    tiles = D // tile
    half = tiles // 2
    assert chunks == 2 and half >= 4
    hops = [functools.partial(tok_step, k) for k in range(H)]
    first = [functools.partial(ig_hop, 0, k) for k in range(H + 1)] + [functools.partial(ig_end, 0)]
    second = [functools.partial(ig_hop, 1, k) for k in range(H + 1)] + [functools.partial(ig_end, 1)]
    for t in range(half):
        blend_rows(t * tile, (t + 1) * tile)
        if t % 2 == 0:
            hops.pop(0)()
    for copy in cots:
        copy.wait_recv()
    ig_dot(0)
    hops.pop(0)()
    low, high = range(lanes // 2), range(lanes // 2, lanes)
    outs = []
    for some in (low, high):
        for t in range(half, tiles, 2):
            blend_rows(t * tile, (t + 2) * tile, some)
            if hops:
                hops.pop(0)()
            first.pop(0)()
        if some is low:
            while hops:
                hops.pop(0)()
            for copy in sibs:
                copy.wait_recv()
            outs += out_dot(0, 2)
    ig_dot(1)
    first.pop(0)()
    outs += out_dot(1, 2)
    for t in range(tiles):
        if first and t == 1:
            first.pop(0)()
        if t % 2 == 0:
            second.pop(0)()
        grad_rows(t)
    for pending in (first, second):
        while pending:
            pending.pop(0)()
    for b in range(3):
        total = jnp.sum(sums[b], axis=0, keepdims=True)
        for i in range(lanes):
            trb[r, b, i : i + 1, :] = total[:, i * 128 : (i + 1) * 128]
    terms = [
        send(trb.at[r], trb.at[r], row_send.at[4, k], row_recv.at[4, k], ((r + k) % R, col)) for k in range(1, R)
    ]
    out_end(outs)
    for copy in terms:
        copy.wait_recv()
    total = trb[0]
    for i in range(1, R):
        total = total + trb[i]
    for i in range(lanes):
        cs = pl.ds(i * 128, 128)
        scaled = [coef[8 + b : 9 + b, cs] * total[b, i : i + 1, :] for b in range(3)]
        share = [coef[11 + b : 12 + b, cs] for b in range(3)]
        mean = share[0] * scaled[0] + share[1] * scaled[1] + share[2] * scaled[2]
        for b in range(3):
            lg_out[b : b + 1, cs] = share[b] * (mean - scaled[b])
    for copy in sent:
        copy.wait_send()
    for copy in grads:
        copy.wait()


def place(cuts, *refs):
    sources, targets, held, come, gone = refs[:4], refs[4:8], refs[8:12], refs[12], refs[13]
    steps = []
    for n, src, dst, mid in zip(cuts, sources, targets, held):
        rows = src.shape[0] // n
        for k in range(n):
            cut = pl.ds(k * rows, rows)
            i = len(steps)
            steps.append(
                (
                    pltpu.make_async_copy(src.at[cut], mid.at[cut], come.at[i]),
                    pltpu.make_async_copy(mid.at[cut], dst.at[cut], gone.at[i]),
                )
            )
            steps[-1][0].start()
    for into, out in steps:
        into.wait()
        out.start()
    for _, out in steps:
        out.wait()


def shards(R, Z, tokens, weight, logits, cotangent):
    D, F = weight.shape
    H = Z // 2
    chunks, tile = 2, min(256, D // 8)
    T = 2 * Z * 32
    rows = cotangent.shape[0]
    n_w = 4
    vmem = pltpu.VMEM
    dma = pltpu.SemaphoreType.DMA
    scratch = [
        vmem((D, F), BF16), vmem((D, F), F32), vmem((D, F), F32), vmem((D, F), F32), vmem((D, F), F32),
        vmem((2, Z, 32, D), BF16), vmem((2, R, 32, F), BF16), vmem((16, F), F32),
        vmem((R, F // 128, 128), F32), vmem((R, 3, F // 128, 128), F32), vmem((3, 8, F), F32),
        vmem((Z, 32, D), BF16), vmem((Z, 32, D), BF16), vmem((Z, 32, D), F32),
        vmem((H, 32, D), BF16), vmem((H, 32, D), BF16), vmem((H, 32, D), BF16), vmem((H, 32, D), BF16),
        vmem((2, 16, D), BF16), vmem((16, D), BF16),
        vmem((R, rows, F), BF16), vmem((R, rows, F), BF16),
        dma((n_w,)), dma((5,)), dma((D // tile,)), dma((5, R)), dma((5, R)),
        dma((2 + 2 * H,)), dma((2 + 2 * H,)), dma((2, H)), dma((2, H)),
        dma((chunks, 2 + 2 * H)), dma((chunks, 2 + 2 * H)),
    ]
    results = pl.pallas_call(
        functools.partial(body, R, Z, chunks, tile),
        out_shape=(
            jax.ShapeDtypeStruct((rows, F), BF16),
            jax.ShapeDtypeStruct((16, D), BF16),
            jax.ShapeDtypeStruct((D, F), BF16),
            jax.ShapeDtypeStruct((3, F), F32),
        ),
        in_specs=[
            pl.BlockSpec(memory_space=pl.ANY), pl.BlockSpec(memory_space=pl.ANY),
            pl.BlockSpec(memory_space=vmem), pl.BlockSpec(memory_space=pl.ANY),
        ],
        out_specs=(
            pl.BlockSpec(memory_space=vmem), pl.BlockSpec(memory_space=vmem),
            pl.BlockSpec(memory_space=pl.ANY), pl.BlockSpec(memory_space=vmem),
        ),
        scratch_shapes=scratch,
        compiler_params=pltpu.CompilerParams(
            collective_id=0, has_side_effects=True, vmem_limit_bytes=59 * 2**20
        ),
    )(tokens, weight, logits, cotangent)
    cuts = (1, 1, 8, 1)
    return pl.pallas_call(
        functools.partial(place, cuts),
        out_shape=tuple(jax.ShapeDtypeStruct(v.shape, v.dtype) for v in results),
        in_specs=[pl.BlockSpec(memory_space=pl.ANY)] * 4,
        out_specs=[pl.BlockSpec(memory_space=pl.ANY)] * 4,
        scratch_shapes=[vmem(v.shape, v.dtype) for v in results] + [dma((sum(cuts),)), dma((sum(cuts),))],
    )(*results)


def solution(mesh):
    R, Z = mesh.shape["row"], mesh.shape["col"] // 4
    in_specs = (P("col", "row"), P("row", "col"), P(None, "col"), P("row", "col"))
    out_specs = (P("row", "col"), P("col", "row"), P("row", "col"), P(None, "col"))
    return jax.shard_map(
        functools.partial(shards, R, Z), mesh=mesh, in_specs=in_specs, out_specs=out_specs, check_vma=False
    )
```

```python
import functools

import jax
import jax.numpy as jnp
from jax import lax
from jax.experimental import pallas as pl
from jax.experimental.pallas import tpu as pltpu
from jax.sharding import PartitionSpec as P

EPSILON = 1e-06
LEVELS = (1.0, 7.0, 127.0)
PI = 3.141592653589793
MESH = pl.DeviceIdType.MESH
F32, BF16 = jnp.float32, jnp.bfloat16

SIN_FINE = (
    3.1415927410125732, -5.167709827423096, 2.550069808959961, -0.5982421040534973, 0.07756038755178452,
)
COS_FINE = (
    0.9999999403953552, -4.934792995452881, 4.058412075042725, -1.3318802118301392, 0.2196968048810959,
)
SIN_WIDE = (3.141589641571045, -5.167367935180664, 2.543604850769043, -0.55839604139328)


def monic(coefficients):
    lead = coefficients[-1]
    return lead, tuple(c / lead for c in coefficients[:-1])


SIN0_LEAD, SIN0 = monic(SIN_FINE)
COS0_LEAD, COS0 = monic(COS_FINE)
SIN2_LEAD, SIN2 = monic(SIN_WIDE)
COS2_LEAD, COS2 = monic(COS_FINE)
Q = SIN0_LEAD * SIN0_LEAD
SIN1_LEAD, SIN1 = monic((7.0, -56.0 * Q, 112.0 * Q**2, -64.0 * Q**3))
COS1_LEAD, COS1 = monic((1.0, -24.0 * Q, 80.0 * Q**2, -64.0 * Q**3))
SIN_SCALE = (SIN0_LEAD, SIN0_LEAD * SIN1_LEAD, SIN2_LEAD)
COS_SCALE = (COS0_LEAD, COS0_LEAD * COS1_LEAD, COS2_LEAD)


def horner(coefficients, x):
    total = x + coefficients[-1]
    for c in coefficients[-2::-1]:
        total = total * x + c
    return total


def soft_round(w, inv0, inv2, blend, slope):
    u0 = w * inv0
    r0 = u0 - jnp.round(u0)
    t0 = r0 * r0
    s0 = r0 * horner(SIN0, t0)
    c0 = horner(COS0, t0)
    z0 = s0 * s0
    p0 = s0 * c0
    s1 = s0 * horner(SIN1, z0)
    c1 = c0 * horner(COS1, z0)
    p1 = s1 * c1
    u2 = w * inv2
    r2 = u2 - jnp.round(u2)
    t2 = r2 * r2
    s2 = r2 * horner(SIN2, t2)
    c2 = horner(COS2, t2)
    p2 = s2 * c2
    blended = w - (blend[0] * p0 + blend[1] * p1 + blend[2] * p2)
    slopes = slope[0] * z0 + slope[1] * (s1 * s1) + slope[2] * (s2 * s2)
    return blended, slopes, p0, p1, p2


def body(
    R, Z, chunks, tile,
    tok_in, w_in, logits, cot_in,
    mixed_out, input_out, wg_out, lg_out,
    wv, slo, pr0, pr1, pr2, tokb, cotb, coef, pkb, trb, sums,
    igs, igr, own, rs_r, rs_l, rr_r, rr_l, zs, zr, xs, xr, ots, otr,
    w_sem, loc_sem, wo_sem, row_send, row_recv, tok_send, tok_recv, ring_send, ring_recv,
    ig_send, ig_recv,
):
    D, F = wv.shape
    H = Z // 2
    r = lax.axis_index("row")
    col = lax.axis_index("col")
    z, xh, c = col // 4, (col // 2) % 2, col % 2
    right = (r, ((z + 1) % Z) * 4 + xh * 2 + c)
    left = (r, ((z + Z - 1) % Z) * 4 + xh * 2 + c)
    across = (r, z * 4 + (1 - xh) * 2 + c)
    sibling = (r, z * 4 + xh * 2 + (1 - c))
    sent = []

    def send(src, dst, ssem, rsem, to):
        copy = pltpu.make_async_remote_copy(
            src_ref=src, dst_ref=dst, send_sem=ssem, recv_sem=rsem, device_id=to, device_id_type=MESH
        )
        copy.start()
        sent.append(copy)
        return copy

    def plane(which):
        return (which + 2 * Z) % Z

    barrier = pltpu.get_barrier_semaphore()
    partners = [((r + k) % R, col) for k in range(1, R)] + [(r, ((z + k) % Z) * 4 + xh * 2 + c) for k in range(1, Z)]
    partners += [across, sibling]
    for to in partners:
        pl.semaphore_signal(barrier, inc=1, device_id=to, device_id_type=MESH)
    n_w = w_sem.shape[0]
    w_rows = D // n_w
    w_copies = []
    own_tok = pltpu.make_async_copy(tok_in, tokb.at[c, z, pl.ds(xh * 16, 16)], loc_sem.at[0])
    own_tok.start()
    own_cot = []
    for a in range(2):
        for b in range(2):
            copy = pltpu.make_async_copy(
                cot_in.at[pl.ds((a * 2 + b) * 16, 16)], cotb.at[b, r, pl.ds(a * 16, 16)], loc_sem.at[1 + a * 2 + b]
            )
            copy.start()
            own_cot.append(copy)
    for k in range(n_w):
        rows = pl.ds(k * w_rows, w_rows)
        copy = pltpu.make_async_copy(w_in.at[rows], wv.at[rows], w_sem.at[k])
        copy.start()
        w_copies.append(copy)
    pl.semaphore_wait(barrier, len(partners))

    own_tok.wait()
    mine = tokb.at[c, z, pl.ds(xh * 16, 16)]
    tok_x = send(mine, mine, tok_send.at[0], tok_recv.at[0], across)

    best = jnp.zeros((16, F), BF16)
    for k in range(n_w):
        w_copies[k].wait()

        def step(i, best, k=k):
            rows = pl.ds(pl.multiple_of(k * w_rows + i * 16, 16), 16)
            return jnp.maximum(best, jnp.abs(wv[rows, :]))

        best = lax.fori_loop(0, w_rows // 16, step, best)
    local = jnp.max(best.astype(F32), axis=0, keepdims=True)
    lanes = F // 128
    for i in range(lanes):
        pkb[r, i : i + 1, :] = local[:, i * 128 : (i + 1) * 128]
    peaks = [
        send(pkb.at[r], pkb.at[r], row_send.at[1, k], row_recv.at[1, k], ((r + k) % R, col)) for k in range(1, R)
    ]

    tok_x.wait_recv()
    piece = tokb.at[c, z]
    sib0 = send(piece, piece, tok_send.at[1], tok_recv.at[1], sibling)
    tok_r = [send(piece, piece, ring_send.at[0, 0], ring_recv.at[0, 0], right)]
    tok_l = [send(piece, piece, ring_send.at[1, 0], ring_recv.at[1, 0], left)]
    sibs = [sib0]

    def tok_step(k):
        tok_r[k].wait_recv()
        tok_l[k].wait_recv()
        half = k == H - 1
        from_left, from_right = plane(z - k - 1), plane(z + k + 1)
        if not half:
            a, b = tokb.at[c, from_left], tokb.at[c, from_right]
            if k == H - 2:
                fa, fb = tokb.at[c, from_left, pl.ds(0, 16)], tokb.at[c, from_right, pl.ds(16, 16)]
            else:
                fa, fb = a, b
            tok_r.append(send(fa, fa, ring_send.at[0, k + 1], ring_recv.at[0, k + 1], right))
            tok_l.append(send(fb, fb, ring_send.at[1, k + 1], ring_recv.at[1, k + 1], left))
            sibs.append(send(a, a, tok_send.at[2 + 2 * k], tok_recv.at[2 + 2 * k], sibling))
            sibs.append(send(b, b, tok_send.at[3 + 2 * k], tok_recv.at[3 + 2 * k], sibling))
        else:
            a = tokb.at[c, from_left]
            sibs.append(send(a, a, tok_send.at[2 + 2 * k], tok_recv.at[2 + 2 * k], sibling))

    scores = logits[...]
    top = jnp.max(scores, axis=0, keepdims=True)
    raised = jnp.exp(scores - top)
    shares = raised / jnp.sum(raised, axis=0, keepdims=True)
    for copy in peaks:
        copy.wait_recv()
    for copy in own_cot:
        copy.wait()
    cots = [
        send(cotb.at[:, r], cotb.at[:, r], row_send.at[0, k], row_recv.at[0, k], ((r + k) % R, col))
        for k in range(1, R)
    ]
    peak8 = pkb[0]
    for i in range(1, R):
        peak8 = jnp.maximum(peak8, pkb[i])
    for i in range(lanes):
        coef[0:1, i * 128 : (i + 1) * 128] = peak8[i : i + 1, :]
    padded = coef[0:1, :] + EPSILON
    coef[0:1, :] = LEVELS[0] / padded
    coef[1:2, :] = LEVELS[2] / padded
    for b in range(3):
        share = shares[b : b + 1]
        factor = (padded / LEVELS[b]) * (SIN_SCALE[b] * COS_SCALE[b] / PI)
        coef[2 + b : 3 + b, :] = share * factor
        coef[5 + b : 6 + b, :] = share * (2.0 * SIN_SCALE[b] * SIN_SCALE[b])
        coef[8 + b : 9 + b, :] = factor
        coef[11 + b : 12 + b, :] = share

    rows_a = 64

    def blend_rows(first, last, some=None):
        for lane in some or range(lanes):
            cs = pl.ds(lane * 128, 128)
            k = [jnp.broadcast_to(coef[i : i + 1, cs], (rows_a, 128)) for i in range(8)]

            def step(i, carry, cs=cs, k=k):
                rs = pl.ds(pl.multiple_of(i * rows_a, rows_a), rows_a)
                w = wv[rs, cs].astype(F32)
                blended, slopes, p0, p1, p2 = soft_round(w, k[0], k[1], k[2:5], k[5:8])
                wv[rs, cs] = blended.astype(BF16)
                slo[rs, cs] = slopes
                pr0[rs, cs] = p0
                pr1[rs, cs] = p1
                pr2[rs, cs] = p2
                return carry

            lax.fori_loop(first // rows_a, last // rows_a, step, 0)

    NT = (((1,), (1,)), ((), ()))
    starts = [sum(chunks[:q]) for q in range(len(chunks))]
    chains = [dict() for _ in chunks]

    def ig_dot(q):
        def step(i, carry):
            rs = pl.ds(pl.multiple_of(starts[q] + i * tile, tile), tile)
            blend = wv[rs, :]
            theirs = lax.dot_general(
                cotb[1 - c].reshape(Z * 32, F), blend, NT, preferred_element_type=F32
            )
            igs[:, :, rs] = theirs.astype(BF16).reshape(Z, 32, tile)
            ours = lax.dot_general(cotb[c].reshape(Z * 32, F), blend, NT, preferred_element_type=F32)
            own[:, :, rs] = ours.reshape(Z, 32, tile)
            return carry

        lax.fori_loop(0, chunks[q] // tile, step, 0)
        cs = pl.ds(starts[q], chunks[q])
        chains[q]["core"] = send(
            igs.at[:, :, cs], igr.at[:, :, cs], ig_send.at[q, 0], ig_recv.at[q, 0], sibling
        )

    def ig_spread(q):
        cs, zc = pl.ds(starts[q], chunks[q]), pl.ds(starts[q] - chunks[0], chunks[q])
        chains[q]["core"].wait_recv()
        chains[q]["z"] = []
        for k in range(1, Z):
            to = (z + k) % Z
            zs[to, :, zc] = (own[to, :, cs] + igr[to, :, cs].astype(F32)).astype(BF16)
            chains[q]["z"].append(
                send(
                    zs.at[to, :, zc], zr.at[z, :, zc], ig_send.at[q, k], ig_recv.at[q, k],
                    (r, to * 4 + xh * 2 + c),
                )
            )

    def ig_gather(q):
        cs, zc = pl.ds(starts[q], chunks[q]), pl.ds(starts[q] - chunks[0], chunks[q])
        for copy in chains[q]["z"]:
            copy.wait_recv()
        total = own[z, :, cs] + igr[z, :, cs].astype(F32)
        for k in range(1, Z):
            total = total + zr[(z + k) % Z, :, zc].astype(F32)
        own[z, :, cs] = total
        for p in range(2):
            xs[p, :, cs] = total[p * 16 : (p + 1) * 16].astype(BF16)
        ig_across(q)

    def ig_across(q):
        cs = pl.ds(starts[q], chunks[q])
        chains[q]["x"] = send(
            xs.at[1 - xh, :, cs], xr.at[:, cs], ig_send.at[q, 1 + 2 * H], ig_recv.at[q, 1 + 2 * H], across
        )

    def ig_hop(q, k):
        cs = pl.ds(starts[q], chunks[q])
        chain = chains[q]
        if k == 0:
            chain["core"].wait_recv()
        else:
            chain["r"].wait_recv()
            chain["l"].wait_recv()

        def term(which, first, count):
            rows = pl.ds(first, count)
            return own[which, rows, cs] + igr[which, rows, cs].astype(F32)

        if k == 0:
            rs_r[0, 0:16, cs] = term(plane(z + H), 0, 16).astype(BF16)
            rs_l[0, 0:16, cs] = term(plane(z + H), 16, 16).astype(BF16)
        elif k == 1 and H > 1:
            for buf, got, to, a in ((rs_r, rr_r, z + H - 1, 0), (rs_l, rr_l, z - H + 1, 16)):
                buf[1, pl.ds(a, 16), cs] = (
                    term(plane(to), a, 16) + got[0, 0:16, cs].astype(F32)
                ).astype(BF16)
                buf[1, pl.ds(16 - a, 16), cs] = term(plane(to), 16 - a, 16).astype(BF16)
        elif k < H:
            for buf, got, to in ((rs_r, rr_r, z + H - k), (rs_l, rr_l, z - H + k)):
                buf[k, :, cs] = (term(plane(to), 0, 32) + got[k - 1, :, cs].astype(F32)).astype(BF16)
        if k < H:
            rows = pl.ds(0, 16 if k == 0 else 32)
            for name, buf, got, to, d in (("r", rs_r, rr_r, right, 0), ("l", rs_l, rr_l, left, 1)):
                chain[name] = send(
                    buf.at[k, rows, cs], got.at[k, rows, cs],
                    ig_send.at[q, 1 + 2 * k + d], ig_recv.at[q, 1 + 2 * k + d], to,
                )
        else:
            for p in range(2):
                rows = pl.ds(p * 16, 16)
                total = term(z, p * 16, 16)
                if H > 1:
                    total = total + (rr_r[H - 1, rows, cs].astype(F32) + rr_l[H - 1, rows, cs].astype(F32))
                else:
                    total = total + (rr_r, rr_l)[p][0, 0:16, cs].astype(F32)
                own[z, rows, cs] = total
                xs[p, :, cs] = total.astype(BF16)
            ig_across(q)

    def ig_end(q):
        cs = pl.ds(starts[q], chunks[q])
        chains[q]["x"].wait_recv()
        total = own[z, pl.ds(pl.multiple_of(xh * 16, 16), 16), cs] + xr[:, cs].astype(F32)
        input_out[:, cs] = total.astype(BF16)

    def out_dot(part_of, parts):
        span = F // parts

        def step(i, carry):
            cs = pl.ds(pl.multiple_of(part_of * span + i * tile, tile), tile)
            part = jnp.dot(
                tokb[...].reshape(2 * Z * 32, D), wv[:, cs], preferred_element_type=F32
            ).astype(BF16)
            part = part.reshape(2, Z, 32, tile)
            for a in range(2):
                ots[:, pl.ds(a * 32, 32), cs] = part[a]
            return carry

        lax.fori_loop(0, span // tile, step, 0)
        cs = pl.ds(part_of * span, span)
        return [
            send(
                ots.at[(r + k) % R, :, cs], otr.at[r, :, cs],
                row_send.at[2 + part_of, k], row_recv.at[2 + part_of, k], ((r + k) % R, col),
            )
            for k in range(1, R)
        ]

    def out_end(copies):
        for copy in copies:
            copy.wait_recv()
        otr[r] = ots[r]
        for a in range(2):
            for b in range(2):
                rows = pl.ds(a * 32 + b * 16, 16)
                total = otr[0, rows, :].astype(F32)
                for i in range(1, R):
                    total = total + otr[i, rows, :].astype(F32)
                mixed_out[pl.ds((b * 2 + a) * 16, 16), :] = total.astype(BF16)

    grads = []

    def grad_rows(t):
        rs = pl.ds(t * tile, tile)
        turned = tokb[:, :, :, rs].reshape(2 * Z * 32, tile).T

        for i in range(F // tile):
            cs = pl.ds(i * tile, tile)
            mg = jnp.dot(
                turned, cotb[:, :, :, cs].reshape(2 * Z * 32, tile), preferred_element_type=F32
            )
            wv[rs, cs] = (mg * slo[rs, cs]).astype(BF16)
            for b, pr in enumerate((pr0, pr1, pr2)):
                part = jnp.sum((mg * pr[rs, cs]).reshape(tile // 8, 8, tile), axis=0)
                sums[b, :, cs] = part if t == 0 else sums[b, :, cs] + part
        copy = pltpu.make_async_copy(wv.at[rs], wg_out.at[rs], wo_sem.at[t])
        copy.start()
        grads.append(copy)

    tiles = D // tile
    assert tiles == 8 and H == 4
    low, high = range(lanes // 2), range(lanes // 2, lanes)

    def blend(first, last, some=None):
        blend_rows(first * tile, last * tile, some)

    blend(0, 1)
    tok_step(0)
    blend(1, 3)
    tok_step(1)
    blend(3, 5)
    tok_step(2)
    blend(5, 6)
    for copy in cots:
        copy.wait_recv()
    ig_dot(0)
    tok_step(3)
    blend(6, 8, low)
    ig_hop(0, 0)
    for copy in sibs:
        copy.wait_recv()
    outs = out_dot(0, 2)
    ig_dot(1)
    blend(6, 8, high)
    ig_hop(0, 1)
    ig_spread(1)
    ig_dot(2)
    outs += out_dot(1, 2)
    ig_spread(2)
    grad_rows(0)
    ig_hop(0, 2)
    for t in range(1, 4):
        grad_rows(t)
    ig_hop(0, 3)
    ig_gather(1)
    for t in range(4, 7):
        grad_rows(t)
    ig_hop(0, 4)
    grad_rows(7)
    for b in range(3):
        total = jnp.sum(sums[b], axis=0, keepdims=True)
        for i in range(lanes):
            trb[r, b, i : i + 1, :] = total[:, i * 128 : (i + 1) * 128]
    terms = [
        send(trb.at[r], trb.at[r], row_send.at[4, k], row_recv.at[4, k], ((r + k) % R, col)) for k in range(1, R)
    ]
    ig_gather(2)
    ig_end(0)
    ig_end(1)
    out_end(outs)
    ig_end(2)
    for copy in terms:
        copy.wait_recv()
    total = trb[0]
    for i in range(1, R):
        total = total + trb[i]
    for i in range(lanes):
        cs = pl.ds(i * 128, 128)
        scaled = [coef[8 + b : 9 + b, cs] * total[b, i : i + 1, :] for b in range(3)]
        share = [coef[11 + b : 12 + b, cs] for b in range(3)]
        mean = share[0] * scaled[0] + share[1] * scaled[1] + share[2] * scaled[2]
        for b in range(3):
            lg_out[b : b + 1, cs] = share[b] * (mean - scaled[b])
    for copy in sent:
        copy.wait_send()
    for copy in grads:
        copy.wait()


def place(cuts, *refs):
    sources, targets, held, come, gone = refs[:4], refs[4:8], refs[8:12], refs[12], refs[13]
    steps = []
    for n, src, dst, mid in zip(cuts, sources, targets, held):
        rows = src.shape[0] // n
        for k in range(n):
            cut = pl.ds(k * rows, rows)
            i = len(steps)
            steps.append(
                (
                    pltpu.make_async_copy(src.at[cut], mid.at[cut], come.at[i]),
                    pltpu.make_async_copy(mid.at[cut], dst.at[cut], gone.at[i]),
                )
            )
            steps[-1][0].start()
    for into, out in steps:
        into.wait()
        out.start()
    for _, out in steps:
        out.wait()


def shards(R, Z, tokens, weight, logits, cotangent):
    D, F = weight.shape
    H = Z // 2
    tile = D // 8
    chunks = (D // 2, D // 4, D // 4)
    C = chunks[0]
    T = 2 * Z * 32
    rows = cotangent.shape[0]
    n_w = 4
    vmem = pltpu.VMEM
    dma = pltpu.SemaphoreType.DMA
    scratch = [
        vmem((D, F), BF16), vmem((D, F), F32), vmem((D, F), F32), vmem((D, F), F32), vmem((D, F), F32),
        vmem((2, Z, 32, D), BF16), vmem((2, R, 32, F), BF16), vmem((16, F), F32),
        vmem((R, F // 128, 128), F32), vmem((R, 3, F // 128, 128), F32), vmem((3, 8, F), F32),
        vmem((Z, 32, D), BF16), vmem((Z, 32, D), BF16), vmem((Z, 32, D), F32),
        vmem((H, 32, C), BF16), vmem((H, 32, C), BF16), vmem((H, 32, C), BF16), vmem((H, 32, C), BF16),
        vmem((Z, 32, D - C), BF16), vmem((Z, 32, D - C), BF16),
        vmem((2, 16, D), BF16), vmem((16, D), BF16),
        vmem((R, rows, F), BF16), vmem((R, rows, F), BF16),
        dma((n_w,)), dma((5,)), dma((D // tile,)), dma((5, R)), dma((5, R)),
        dma((2 + 2 * H,)), dma((2 + 2 * H,)), dma((2, H)), dma((2, H)),
        dma((len(chunks), 2 + 2 * H)), dma((len(chunks), 2 + 2 * H)),
    ]
    results = pl.pallas_call(
        functools.partial(body, R, Z, chunks, tile),
        out_shape=(
            jax.ShapeDtypeStruct((rows, F), BF16),
            jax.ShapeDtypeStruct((16, D), BF16),
            jax.ShapeDtypeStruct((D, F), BF16),
            jax.ShapeDtypeStruct((3, F), F32),
        ),
        in_specs=[
            pl.BlockSpec(memory_space=pl.ANY), pl.BlockSpec(memory_space=pl.ANY),
            pl.BlockSpec(memory_space=vmem), pl.BlockSpec(memory_space=pl.ANY),
        ],
        out_specs=(
            pl.BlockSpec(memory_space=vmem), pl.BlockSpec(memory_space=vmem),
            pl.BlockSpec(memory_space=pl.ANY), pl.BlockSpec(memory_space=vmem),
        ),
        scratch_shapes=scratch,
        compiler_params=pltpu.CompilerParams(
            collective_id=0, has_side_effects=True, vmem_limit_bytes=59 * 2**20
        ),
    )(tokens, weight, logits, cotangent)
    cuts = (1, 1, 8, 1)
    return pl.pallas_call(
        functools.partial(place, cuts),
        out_shape=tuple(jax.ShapeDtypeStruct(v.shape, v.dtype) for v in results),
        in_specs=[pl.BlockSpec(memory_space=pl.ANY)] * 4,
        out_specs=[pl.BlockSpec(memory_space=pl.ANY)] * 4,
        scratch_shapes=[vmem(v.shape, v.dtype) for v in results] + [dma((sum(cuts),)), dma((sum(cuts),))],
    )(*results)


def solution(mesh):
    R, Z = mesh.shape["row"], mesh.shape["col"] // 4
    in_specs = (P("col", "row"), P("row", "col"), P(None, "col"), P("row", "col"))
    out_specs = (P("row", "col"), P("col", "row"), P("row", "col"), P(None, "col"))
    return jax.shard_map(
        functools.partial(shards, R, Z), mesh=mesh, in_specs=in_specs, out_specs=out_specs, check_vma=False
    )
```

```python
import functools

import jax
import jax.numpy as jnp
from jax import lax
from jax.experimental import pallas as pl
from jax.experimental.pallas import tpu as pltpu
from jax.sharding import PartitionSpec as P

EPSILON = 1e-06
LEVELS = (1.0, 7.0, 127.0)
PI = 3.141592653589793
MESH = pl.DeviceIdType.MESH
F32, BF16 = jnp.float32, jnp.bfloat16

SIN_FINE = (
    3.1415927410125732, -5.167709827423096, 2.550069808959961, -0.5982421040534973, 0.07756038755178452,
)
COS_FINE = (
    0.9999999403953552, -4.934792995452881, 4.058412075042725, -1.3318802118301392, 0.2196968048810959,
)
SIN_WIDE = (3.141589641571045, -5.167367935180664, 2.543604850769043, -0.55839604139328)


def monic(coefficients):
    lead = coefficients[-1]
    return lead, tuple(c / lead for c in coefficients[:-1])


SIN0_LEAD, SIN0 = monic(SIN_FINE)
COS0_LEAD, COS0 = monic(COS_FINE)
SIN2_LEAD, SIN2 = monic(SIN_WIDE)
COS2_LEAD, COS2 = monic(COS_FINE)
Q = SIN0_LEAD * SIN0_LEAD
SIN1_LEAD, SIN1 = monic((7.0, -56.0 * Q, 112.0 * Q**2, -64.0 * Q**3))
COS1_LEAD, COS1 = monic((1.0, -24.0 * Q, 80.0 * Q**2, -64.0 * Q**3))
SIN_SCALE = (SIN0_LEAD, SIN0_LEAD * SIN1_LEAD, SIN2_LEAD)
COS_SCALE = (COS0_LEAD, COS0_LEAD * COS1_LEAD, COS2_LEAD)


def horner(coefficients, x):
    total = x + coefficients[-1]
    for c in coefficients[-2::-1]:
        total = total * x + c
    return total


def soft_round(w, inv0, inv2, blend, slope):
    u0 = w * inv0
    r0 = u0 - jnp.round(u0)
    t0 = r0 * r0
    s0 = r0 * horner(SIN0, t0)
    c0 = horner(COS0, t0)
    z0 = s0 * s0
    p0 = s0 * c0
    s1 = s0 * horner(SIN1, z0)
    c1 = c0 * horner(COS1, z0)
    p1 = s1 * c1
    u2 = w * inv2
    r2 = u2 - jnp.round(u2)
    t2 = r2 * r2
    s2 = r2 * horner(SIN2, t2)
    c2 = horner(COS2, t2)
    p2 = s2 * c2
    blended = w - (blend[0] * p0 + blend[1] * p1 + blend[2] * p2)
    slopes = slope[0] * z0 + slope[1] * (s1 * s1) + slope[2] * (s2 * s2)
    return blended, slopes, p0, p1, p2


def body(
    R, Z, chunks, tile,
    tok_in, w_in, logits, cot_in,
    mixed_out, input_out, wg_out, lg_out,
    wv, slo, pr0, pr1, pr2, tokb, cotb, coef, pkb, trb, sums,
    igs, igr, own, acc, zs, zr, xs, xr, ots, otr, oacc, oxs, oxr,
    w_sem, loc_sem, wo_sem, row_send, row_recv, tok_send, tok_recv, ring_send, ring_recv,
    ig_send, ig_recv,
):
    D, F = wv.shape
    H = Z // 2
    r = lax.axis_index("row")
    col = lax.axis_index("col")
    z, xh, c = col // 4, (col // 2) % 2, col % 2
    right = (r, ((z + 1) % Z) * 4 + xh * 2 + c)
    left = (r, ((z + Z - 1) % Z) * 4 + xh * 2 + c)
    across = (r, z * 4 + (1 - xh) * 2 + c)
    sibling = (r, z * 4 + xh * 2 + (1 - c))
    sent = []

    def send(src, dst, ssem, rsem, to):
        copy = pltpu.make_async_remote_copy(
            src_ref=src, dst_ref=dst, send_sem=ssem, recv_sem=rsem, device_id=to, device_id_type=MESH
        )
        copy.start()
        sent.append(copy)
        return copy

    def plane(which):
        return (which + 2 * Z) % Z

    barrier = pltpu.get_barrier_semaphore()
    partners = [((r + k) % R, col) for k in range(1, R)] + [(r, ((z + k) % Z) * 4 + xh * 2 + c) for k in range(1, Z)]
    partners += [across, sibling]
    for to in partners:
        pl.semaphore_signal(barrier, inc=1, device_id=to, device_id_type=MESH)
    n_w = w_sem.shape[0]
    w_rows = D // n_w
    w_copies = []
    own_tok = pltpu.make_async_copy(tok_in, tokb.at[c, z, pl.ds(xh * 16, 16)], loc_sem.at[0])
    own_tok.start()
    own_cot = []
    for a in range(2):
        for b in range(2):
            copy = pltpu.make_async_copy(
                cot_in.at[pl.ds((a * 2 + b) * 16, 16)], cotb.at[b, r, pl.ds(a * 16, 16)], loc_sem.at[1 + a * 2 + b]
            )
            copy.start()
            own_cot.append(copy)
    for k in range(n_w):
        rows = pl.ds(k * w_rows, w_rows)
        copy = pltpu.make_async_copy(w_in.at[rows], wv.at[rows], w_sem.at[k])
        copy.start()
        w_copies.append(copy)
    pl.semaphore_wait(barrier, len(partners))

    own_tok.wait()
    mine = tokb.at[c, z, pl.ds(xh * 16, 16)]
    tok_x = send(mine, mine, tok_send.at[0], tok_recv.at[0], across)

    best = jnp.zeros((16, F), BF16)
    for k in range(n_w):
        w_copies[k].wait()

        def step(i, best, k=k):
            rows = pl.ds(pl.multiple_of(k * w_rows + i * 16, 16), 16)
            return jnp.maximum(best, jnp.abs(wv[rows, :]))

        best = lax.fori_loop(0, w_rows // 16, step, best)
    local = jnp.max(best.astype(F32), axis=0, keepdims=True)
    lanes = F // 128
    for i in range(lanes):
        pkb[r, i : i + 1, :] = local[:, i * 128 : (i + 1) * 128]
    peaks = [
        send(pkb.at[r], pkb.at[r], row_send.at[1, k], row_recv.at[1, k], ((r + k) % R, col)) for k in range(1, R)
    ]

    tok_x.wait_recv()
    piece = tokb.at[c, z]
    sib0 = send(piece, piece, tok_send.at[1], tok_recv.at[1], sibling)
    tok_r = [send(piece, piece, ring_send.at[0, 0], ring_recv.at[0, 0], right)]
    tok_l = [send(piece, piece, ring_send.at[1, 0], ring_recv.at[1, 0], left)]
    sibs = [sib0]

    def tok_step(k):
        tok_r[k].wait_recv()
        tok_l[k].wait_recv()
        half = k == H - 1
        from_left, from_right = plane(z - k - 1), plane(z + k + 1)
        if not half:
            a, b = tokb.at[c, from_left], tokb.at[c, from_right]
            if k == H - 2:
                fa, fb = tokb.at[c, from_left, pl.ds(0, 16)], tokb.at[c, from_right, pl.ds(16, 16)]
            else:
                fa, fb = a, b
            tok_r.append(send(fa, fa, ring_send.at[0, k + 1], ring_recv.at[0, k + 1], right))
            tok_l.append(send(fb, fb, ring_send.at[1, k + 1], ring_recv.at[1, k + 1], left))
            sibs.append(send(a, a, tok_send.at[2 + 2 * k], tok_recv.at[2 + 2 * k], sibling))
            sibs.append(send(b, b, tok_send.at[3 + 2 * k], tok_recv.at[3 + 2 * k], sibling))
        else:
            a = tokb.at[c, from_left]
            sibs.append(send(a, a, tok_send.at[2 + 2 * k], tok_recv.at[2 + 2 * k], sibling))

    scores = logits[...]
    top = jnp.max(scores, axis=0, keepdims=True)
    raised = jnp.exp(scores - top)
    shares = raised / jnp.sum(raised, axis=0, keepdims=True)
    for copy in peaks:
        copy.wait_recv()
    for copy in own_cot:
        copy.wait()
    cots = [
        send(cotb.at[:, r], cotb.at[:, r], row_send.at[0, k], row_recv.at[0, k], ((r + k) % R, col))
        for k in range(1, R)
    ]
    peak8 = pkb[0]
    for i in range(1, R):
        peak8 = jnp.maximum(peak8, pkb[i])
    for i in range(lanes):
        coef[0:1, i * 128 : (i + 1) * 128] = peak8[i : i + 1, :]
    padded = coef[0:1, :] + EPSILON
    coef[0:1, :] = LEVELS[0] / padded
    coef[1:2, :] = LEVELS[2] / padded
    for b in range(3):
        share = shares[b : b + 1]
        factor = (padded / LEVELS[b]) * (SIN_SCALE[b] * COS_SCALE[b] / PI)
        coef[2 + b : 3 + b, :] = share * factor
        coef[5 + b : 6 + b, :] = share * (2.0 * SIN_SCALE[b] * SIN_SCALE[b])
        coef[8 + b : 9 + b, :] = factor
        coef[11 + b : 12 + b, :] = share

    rows_a = 64

    def blend_rows(first, last, some=None):
        for lane in some or range(lanes):
            cs = pl.ds(lane * 128, 128)
            k = [jnp.broadcast_to(coef[i : i + 1, cs], (rows_a, 128)) for i in range(8)]

            def step(i, carry, cs=cs, k=k):
                rs = pl.ds(pl.multiple_of(i * rows_a, rows_a), rows_a)
                w = wv[rs, cs].astype(F32)
                blended, slopes, p0, p1, p2 = soft_round(w, k[0], k[1], k[2:5], k[5:8])
                wv[rs, cs] = blended.astype(BF16)
                slo[rs, cs] = slopes
                pr0[rs, cs] = p0
                pr1[rs, cs] = p1
                pr2[rs, cs] = p2
                return carry

            lax.fori_loop(first // rows_a, last // rows_a, step, 0)

    NT = (((1,), (1,)), ((), ()))
    starts = [sum(chunks[:q]) for q in range(len(chunks))]
    chains = [dict() for _ in chunks]

    def ig_dot(q):
        def step(i, carry):
            rs = pl.ds(pl.multiple_of(starts[q] + i * tile, tile), tile)
            blend = wv[rs, :]
            theirs = lax.dot_general(
                cotb[1 - c].reshape(Z * 32, F), blend, NT, preferred_element_type=F32
            )
            igs[:, :, rs] = theirs.astype(BF16).reshape(Z, 32, tile)
            ours = lax.dot_general(cotb[c].reshape(Z * 32, F), blend, NT, preferred_element_type=F32)
            own[:, :, rs] = ours.reshape(Z, 32, tile)
            return carry

        lax.fori_loop(0, chunks[q] // tile, step, 0)
        cs = pl.ds(starts[q], chunks[q])
        chains[q]["core"] = send(
            igs.at[:, :, cs], igr.at[:, :, cs], ig_send.at[q, 0], ig_recv.at[q, 0], sibling
        )

    def ig_across(q):
        cs = pl.ds(starts[q], chunks[q])
        chains[q]["core"].wait_recv()
        rows = pl.ds(pl.multiple_of((1 - xh) * 16, 16), 16)
        for k in range(Z):
            xs[k, :, cs] = (own[k, rows, cs] + igr[k, rows, cs].astype(F32)).astype(BF16)
        chains[q]["x"] = send(
            xs.at[:, :, cs], xr.at[:, :, cs], ig_send.at[q, Z], ig_recv.at[q, Z], across
        )

    def ig_spread(q):
        cs = pl.ds(starts[q], chunks[q])
        chains[q]["x"].wait_recv()
        rows = pl.ds(pl.multiple_of(xh * 16, 16), 16)
        chains[q]["z"] = []
        for k in range(Z):
            to = (z + k) % Z
            total = own[to, rows, cs] + (igr[to, rows, cs].astype(F32) + xr[to, :, cs].astype(F32))
            if k == 0:
                acc[:, cs] = total
                continue
            zs[to, :, cs] = total.astype(BF16)
            chains[q]["z"].append(
                send(
                    zs.at[to, :, cs], zr.at[z, :, cs], ig_send.at[q, k], ig_recv.at[q, k],
                    (r, to * 4 + xh * 2 + c),
                )
            )

    def ig_end(q):
        cs = pl.ds(starts[q], chunks[q])
        for copy in chains[q]["z"]:
            copy.wait_recv()
        total = acc[:, cs]
        for k in range(1, Z):
            total = total + zr[(z + k) % Z, :, cs].astype(F32)
        input_out[:, cs] = total.astype(BF16)

    def out_dot(part_of, parts):
        span = F // parts

        def step(i, carry):
            cs = pl.ds(pl.multiple_of(part_of * span + i * tile, tile), tile)
            part = jnp.dot(
                tokb[...].reshape(2 * Z * 32, D), wv[:, cs], preferred_element_type=F32
            ).astype(BF16)
            part = part.reshape(2, Z, 32, tile)
            for a in range(2):
                ots[:, :, pl.ds(a * 32, 32), cs] = part[a].reshape(2, R // 2, 32, tile)
            return carry

        lax.fori_loop(0, span // tile, step, 0)

    side, place_y, ring_y = r // (R // 2), r % (R // 2), R // 2
    outs = [dict(), dict()]

    def out_send(h):
        cs = pl.ds(h * (F // 2), F // 2)
        outs[h]["y"] = []
        for k in range(1, ring_y):
            to = (place_y + k) % ring_y
            outs[h]["y"].append(
                send(
                    ots.at[:, to, :, cs], otr.at[:, place_y, :, cs], row_send.at[2 + h, k], row_recv.at[2 + h, k],
                    (side * ring_y + to, col),
                )
            )

    def out_turn(h):
        cs = pl.ds(h * (F // 2), F // 2)
        for copy in outs[h]["y"]:
            copy.wait_recv()

        def total(which):
            value = ots[which, place_y, :, cs].astype(F32)
            for k in range(1, ring_y):
                value = value + otr[which, (place_y + k) % ring_y, :, cs].astype(F32)
            return value

        oxs[:, cs] = total(1 - side).astype(BF16)
        outs[h]["x"] = send(
            oxs.at[:, cs], oxr.at[:, cs], row_send.at[2 + h, ring_y], row_recv.at[2 + h, ring_y],
            ((1 - side) * ring_y + place_y, col),
        )
        oacc[:, cs] = total(side)

    def out_end(h):
        cs = pl.ds(h * (F // 2), F // 2)
        outs[h]["x"].wait_recv()
        for a in range(2):
            for b in range(2):
                rows = pl.ds(a * 32 + b * 16, 16)
                value = oacc[rows, cs] + oxr[rows, cs].astype(F32)
                mixed_out[pl.ds((b * 2 + a) * 16, 16), cs] = value.astype(BF16)

    grads = []

    def grad_rows(t):
        rs = pl.ds(t * tile, tile)
        turned = tokb[:, :, :, rs].reshape(2 * Z * 32, tile).T

        for i in range(F // tile):
            cs = pl.ds(i * tile, tile)
            mg = jnp.dot(
                turned, cotb[:, :, :, cs].reshape(2 * Z * 32, tile), preferred_element_type=F32
            )
            wv[rs, cs] = (mg * slo[rs, cs]).astype(BF16)
            for b, pr in enumerate((pr0, pr1, pr2)):
                part = jnp.sum((mg * pr[rs, cs]).reshape(tile // 8, 8, tile), axis=0)
                sums[b, :, cs] = part if t == 0 else sums[b, :, cs] + part
        copy = pltpu.make_async_copy(wv.at[rs], wg_out.at[rs], wo_sem.at[t])
        copy.start()
        grads.append(copy)

    tiles = D // tile
    assert tiles == 8 and H == 4
    low, high = range(lanes // 2), range(lanes // 2, lanes)

    def blend(first, last, some=None):
        blend_rows(first * tile, last * tile, some)

    blend(0, 1)
    tok_step(0)
    blend(1, 3)
    tok_step(1)
    blend(3, 5)
    tok_step(2)
    blend(5, 6)
    for copy in cots:
        copy.wait_recv()
    ig_dot(0)
    tok_step(3)
    blend(6, 8, low)
    ig_across(0)
    for copy in sibs:
        copy.wait_recv()
    out_dot(0, 2)
    out_send(0)
    ig_dot(1)
    blend(6, 8, high)
    ig_across(1)
    ig_dot(2)
    out_dot(1, 2)
    ig_across(2)
    out_send(1)
    grad_rows(0)
    ig_spread(0)
    grad_rows(1)
    grad_rows(2)
    out_turn(0)
    grad_rows(3)
    grad_rows(4)
    ig_spread(1)
    for t in range(5, 8):
        grad_rows(t)
    for b in range(3):
        total = jnp.sum(sums[b], axis=0, keepdims=True)
        for i in range(lanes):
            trb[r, b, i : i + 1, :] = total[:, i * 128 : (i + 1) * 128]
    terms = [
        send(trb.at[r], trb.at[r], row_send.at[4, k], row_recv.at[4, k], ((r + k) % R, col)) for k in range(1, R)
    ]
    ig_spread(2)
    out_turn(1)
    out_end(0)
    ig_end(0)
    ig_end(1)
    for copy in terms:
        copy.wait_recv()
    total = trb[0]
    for i in range(1, R):
        total = total + trb[i]
    for i in range(lanes):
        cs = pl.ds(i * 128, 128)
        scaled = [coef[8 + b : 9 + b, cs] * total[b, i : i + 1, :] for b in range(3)]
        share = [coef[11 + b : 12 + b, cs] for b in range(3)]
        mean = share[0] * scaled[0] + share[1] * scaled[1] + share[2] * scaled[2]
        for b in range(3):
            lg_out[b : b + 1, cs] = share[b] * (mean - scaled[b])
    out_end(1)
    ig_end(2)
    for copy in sent:
        copy.wait_send()
    for copy in grads:
        copy.wait()


def place(cuts, *refs):
    sources, targets, held, come, gone = refs[:4], refs[4:8], refs[8:12], refs[12], refs[13]
    steps = []
    for n, src, dst, mid in zip(cuts, sources, targets, held):
        rows = src.shape[0] // n
        for k in range(n):
            cut = pl.ds(k * rows, rows)
            i = len(steps)
            steps.append(
                (
                    pltpu.make_async_copy(src.at[cut], mid.at[cut], come.at[i]),
                    pltpu.make_async_copy(mid.at[cut], dst.at[cut], gone.at[i]),
                )
            )
            steps[-1][0].start()
    for into, out in steps:
        into.wait()
        out.start()
    for _, out in steps:
        out.wait()


def shards(R, Z, tokens, weight, logits, cotangent):
    D, F = weight.shape
    H = Z // 2
    tile = D // 8
    chunks = (D // 2, D // 4, D // 4)
    T = 2 * Z * 32
    rows = cotangent.shape[0]
    n_w = 4
    vmem = pltpu.VMEM
    dma = pltpu.SemaphoreType.DMA
    scratch = [
        vmem((D, F), BF16), vmem((D, F), F32), vmem((D, F), F32), vmem((D, F), F32), vmem((D, F), F32),
        vmem((2, Z, 32, D), BF16), vmem((2, R, 32, F), BF16), vmem((16, F), F32),
        vmem((R, F // 128, 128), F32), vmem((R, 3, F // 128, 128), F32), vmem((3, 8, F), F32),
        vmem((Z, 32, D), BF16), vmem((Z, 32, D), BF16), vmem((Z, 32, D), F32),
        vmem((16, D), F32), vmem((Z, 16, D), BF16), vmem((Z, 16, D), BF16), vmem((Z, 16, D), BF16), vmem((Z, 16, D), BF16),
        vmem((2, R // 2, rows, F), BF16), vmem((2, R // 2, rows, F), BF16),
        vmem((rows, F), F32), vmem((rows, F), BF16), vmem((rows, F), BF16),
        dma((n_w,)), dma((5,)), dma((D // tile,)), dma((5, R)), dma((5, R)),
        dma((2 + 2 * H,)), dma((2 + 2 * H,)), dma((2, H)), dma((2, H)),
        dma((len(chunks), 2 + 2 * H)), dma((len(chunks), 2 + 2 * H)),
    ]
    results = pl.pallas_call(
        functools.partial(body, R, Z, chunks, tile),
        out_shape=(
            jax.ShapeDtypeStruct((rows, F), BF16),
            jax.ShapeDtypeStruct((16, D), BF16),
            jax.ShapeDtypeStruct((D, F), BF16),
            jax.ShapeDtypeStruct((3, F), F32),
        ),
        in_specs=[
            pl.BlockSpec(memory_space=pl.ANY), pl.BlockSpec(memory_space=pl.ANY),
            pl.BlockSpec(memory_space=vmem), pl.BlockSpec(memory_space=pl.ANY),
        ],
        out_specs=(
            pl.BlockSpec(memory_space=vmem), pl.BlockSpec(memory_space=vmem),
            pl.BlockSpec(memory_space=pl.ANY), pl.BlockSpec(memory_space=vmem),
        ),
        scratch_shapes=scratch,
        compiler_params=pltpu.CompilerParams(
            collective_id=0, has_side_effects=True, vmem_limit_bytes=59 * 2**20
        ),
    )(tokens, weight, logits, cotangent)
    cuts = (1, 1, 8, 1)
    return pl.pallas_call(
        functools.partial(place, cuts),
        out_shape=tuple(jax.ShapeDtypeStruct(v.shape, v.dtype) for v in results),
        in_specs=[pl.BlockSpec(memory_space=pl.ANY)] * 4,
        out_specs=[pl.BlockSpec(memory_space=pl.ANY)] * 4,
        scratch_shapes=[vmem(v.shape, v.dtype) for v in results] + [dma((sum(cuts),)), dma((sum(cuts),))],
    )(*results)


def solution(mesh):
    R, Z = mesh.shape["row"], mesh.shape["col"] // 4
    in_specs = (P("col", "row"), P("row", "col"), P(None, "col"), P("row", "col"))
    out_specs = (P("row", "col"), P("col", "row"), P("row", "col"), P(None, "col"))
    return jax.shard_map(
        functools.partial(shards, R, Z), mesh=mesh, in_specs=in_specs, out_specs=out_specs, check_vma=False
    )
```

```python
import functools

import jax
import jax.numpy as jnp
from jax import lax
from jax.experimental import pallas as pl
from jax.experimental.pallas import tpu as pltpu
from jax.sharding import PartitionSpec as P

EPSILON = 1e-06
LEVELS = (1.0, 7.0, 127.0)
PI = 3.141592653589793
MESH = pl.DeviceIdType.MESH
F32, BF16 = jnp.float32, jnp.bfloat16

SIN_FINE = (
    3.1415927410125732, -5.167709827423096, 2.550069808959961, -0.5982421040534973, 0.07756038755178452,
)
COS_FINE = (
    0.9999999403953552, -4.934792995452881, 4.058412075042725, -1.3318802118301392, 0.2196968048810959,
)
SIN_WIDE = (3.141589641571045, -5.167367935180664, 2.543604850769043, -0.55839604139328)


def monic(coefficients):
    lead = coefficients[-1]
    return lead, tuple(c / lead for c in coefficients[:-1])


SIN0_LEAD, SIN0 = monic(SIN_FINE)
COS0_LEAD, COS0 = monic(COS_FINE)
SIN2_LEAD, SIN2 = monic(SIN_WIDE)
COS2_LEAD, COS2 = monic(COS_FINE)
Q = SIN0_LEAD * SIN0_LEAD
SIN1_LEAD, SIN1 = monic((7.0, -56.0 * Q, 112.0 * Q**2, -64.0 * Q**3))
COS1_LEAD, COS1 = monic((1.0, -24.0 * Q, 80.0 * Q**2, -64.0 * Q**3))
SIN_SCALE = (SIN0_LEAD, SIN0_LEAD * SIN1_LEAD, SIN2_LEAD)
COS_SCALE = (COS0_LEAD, COS0_LEAD * COS1_LEAD, COS2_LEAD)


def horner(coefficients, x):
    total = x + coefficients[-1]
    for c in coefficients[-2::-1]:
        total = total * x + c
    return total


def soft_round(w, inv0, inv2, blend, slope):
    u0 = w * inv0
    r0 = u0 - jnp.round(u0)
    t0 = r0 * r0
    s0 = r0 * horner(SIN0, t0)
    c0 = horner(COS0, t0)
    z0 = s0 * s0
    p0 = s0 * c0
    s1 = s0 * horner(SIN1, z0)
    c1 = c0 * horner(COS1, z0)
    p1 = s1 * c1
    u2 = w * inv2
    r2 = u2 - jnp.round(u2)
    t2 = r2 * r2
    s2 = r2 * horner(SIN2, t2)
    c2 = horner(COS2, t2)
    p2 = s2 * c2
    blended = w - (blend[0] * p0 + blend[1] * p1 + blend[2] * p2)
    slopes = slope[0] * z0 + slope[1] * (s1 * s1) + slope[2] * (s2 * s2)
    return blended, slopes, p0, p1, p2


def body(
    R, Z, chunks, tile,
    tok_in, w_in, logits, cot_in,
    mixed_out, input_out, wg_out, lg_out,
    wv, slo, pr0, pr1, pr2, tokb, cotb, coef, pkb, trb, sums,
    igs, igr, own, acc, zs, zr, xs, xr, ots, otr, oacc, oxs, oxr,
    w_sem, loc_sem, wo_sem, row_send, row_recv, tok_send, tok_recv, ring_send, ring_recv,
    ig_send, ig_recv,
):
    D, F = wv.shape
    H = Z // 2
    r = lax.axis_index("row")
    col = lax.axis_index("col")
    z, xh, c = col // 4, (col // 2) % 2, col % 2
    right = (r, ((z + 1) % Z) * 4 + xh * 2 + c)
    left = (r, ((z + Z - 1) % Z) * 4 + xh * 2 + c)
    across = (r, z * 4 + (1 - xh) * 2 + c)
    sibling = (r, z * 4 + xh * 2 + (1 - c))
    sent = []

    def send(src, dst, ssem, rsem, to):
        copy = pltpu.make_async_remote_copy(
            src_ref=src, dst_ref=dst, send_sem=ssem, recv_sem=rsem, device_id=to, device_id_type=MESH
        )
        copy.start()
        sent.append(copy)
        return copy

    def plane(which):
        return (which + 2 * Z) % Z

    barrier = pltpu.get_barrier_semaphore()
    partners = [((r + k) % R, col) for k in range(1, R)] + [(r, ((z + k) % Z) * 4 + xh * 2 + c) for k in range(1, Z)]
    partners += [across, sibling]
    for to in partners:
        pl.semaphore_signal(barrier, inc=1, device_id=to, device_id_type=MESH)
    n_w = w_sem.shape[0]
    w_rows = D // n_w
    w_copies = []
    own_tok = pltpu.make_async_copy(tok_in, tokb.at[c, z, pl.ds(xh * 16, 16)], loc_sem.at[0])
    own_tok.start()
    own_cot = []
    for a in range(2):
        for b in range(2):
            copy = pltpu.make_async_copy(
                cot_in.at[pl.ds((a * 2 + b) * 16, 16)], cotb.at[b, r, pl.ds(a * 16, 16)], loc_sem.at[1 + a * 2 + b]
            )
            copy.start()
            own_cot.append(copy)
    for k in range(n_w):
        rows = pl.ds(k * w_rows, w_rows)
        copy = pltpu.make_async_copy(w_in.at[rows], wv.at[rows], w_sem.at[k])
        copy.start()
        w_copies.append(copy)
    pl.semaphore_wait(barrier, len(partners))

    own_tok.wait()
    mine = tokb.at[c, z, pl.ds(xh * 16, 16)]
    tok_x = send(mine, mine, tok_send.at[0], tok_recv.at[0], across)

    for copy in own_cot:
        copy.wait()

    def cot_send(k):
        block = cotb.at[:, r]
        return send(block, block, row_send.at[0, k], row_recv.at[0, k], ((r + k) % R, col))

    near = (R // 2, 1, R - 1)
    cots = [cot_send(k) for k in near]

    best = jnp.zeros((16, F), BF16)
    for k in range(n_w):
        w_copies[k].wait()

        def step(i, best, k=k):
            rows = pl.ds(pl.multiple_of(k * w_rows + i * 16, 16), 16)
            return jnp.maximum(best, jnp.abs(wv[rows, :]))

        best = lax.fori_loop(0, w_rows // 16, step, best)
    local = jnp.max(best.astype(F32), axis=0, keepdims=True)
    lanes = F // 128
    for i in range(lanes):
        pkb[r, i : i + 1, :] = local[:, i * 128 : (i + 1) * 128]
    peaks = [
        send(pkb.at[r], pkb.at[r], row_send.at[1, k], row_recv.at[1, k], ((r + k) % R, col)) for k in range(1, R)
    ]

    tok_x.wait_recv()
    piece = tokb.at[c, z]
    sib0 = send(piece, piece, tok_send.at[1], tok_recv.at[1], sibling)
    tok_r = [send(piece, piece, ring_send.at[0, 0], ring_recv.at[0, 0], right)]
    tok_l = [send(piece, piece, ring_send.at[1, 0], ring_recv.at[1, 0], left)]
    sibs = [sib0]

    def tok_step(k):
        tok_r[k].wait_recv()
        tok_l[k].wait_recv()
        half = k == H - 1
        from_left, from_right = plane(z - k - 1), plane(z + k + 1)
        if not half:
            a, b = tokb.at[c, from_left], tokb.at[c, from_right]
            if k == H - 2:
                fa, fb = tokb.at[c, from_left, pl.ds(0, 16)], tokb.at[c, from_right, pl.ds(16, 16)]
            else:
                fa, fb = a, b
            tok_r.append(send(fa, fa, ring_send.at[0, k + 1], ring_recv.at[0, k + 1], right))
            tok_l.append(send(fb, fb, ring_send.at[1, k + 1], ring_recv.at[1, k + 1], left))
            sibs.append(send(a, a, tok_send.at[2 + 2 * k], tok_recv.at[2 + 2 * k], sibling))
            sibs.append(send(b, b, tok_send.at[3 + 2 * k], tok_recv.at[3 + 2 * k], sibling))
        else:
            a = tokb.at[c, from_left]
            sibs.append(send(a, a, tok_send.at[2 + 2 * k], tok_recv.at[2 + 2 * k], sibling))

    scores = logits[...]
    top = jnp.max(scores, axis=0, keepdims=True)
    raised = jnp.exp(scores - top)
    shares = raised / jnp.sum(raised, axis=0, keepdims=True)
    for copy in peaks:
        copy.wait_recv()
    cots += [cot_send(k) for k in range(1, R) if k not in near]
    peak8 = pkb[0]
    for i in range(1, R):
        peak8 = jnp.maximum(peak8, pkb[i])
    for i in range(lanes):
        coef[0:1, i * 128 : (i + 1) * 128] = peak8[i : i + 1, :]
    padded = coef[0:1, :] + EPSILON
    coef[0:1, :] = LEVELS[0] / padded
    coef[1:2, :] = LEVELS[2] / padded
    for b in range(3):
        share = shares[b : b + 1]
        factor = (padded / LEVELS[b]) * (SIN_SCALE[b] * COS_SCALE[b] / PI)
        coef[2 + b : 3 + b, :] = share * factor
        coef[5 + b : 6 + b, :] = share * (2.0 * SIN_SCALE[b] * SIN_SCALE[b])
        coef[8 + b : 9 + b, :] = factor
        coef[11 + b : 12 + b, :] = share

    rows_a = 64

    def blend_rows(first, last, some=None):
        for lane in some or range(lanes):
            cs = pl.ds(lane * 128, 128)
            k = [jnp.broadcast_to(coef[i : i + 1, cs], (rows_a, 128)) for i in range(8)]

            def step(i, carry, cs=cs, k=k):
                rs = pl.ds(pl.multiple_of(i * rows_a, rows_a), rows_a)
                w = wv[rs, cs].astype(F32)
                blended, slopes, p0, p1, p2 = soft_round(w, k[0], k[1], k[2:5], k[5:8])
                wv[rs, cs] = blended.astype(BF16)
                slo[rs, cs] = slopes
                pr0[rs, cs] = p0
                pr1[rs, cs] = p1
                pr2[rs, cs] = p2
                return carry

            lax.fori_loop(first // rows_a, last // rows_a, step, 0)

    NT = (((1,), (1,)), ((), ()))
    starts = [sum(chunks[:q]) for q in range(len(chunks))]
    chains = [dict() for _ in chunks]

    def ig_dot(q):
        def step(i, carry):
            rs = pl.ds(pl.multiple_of(starts[q] + i * tile, tile), tile)
            blend = wv[rs, :]
            theirs = lax.dot_general(
                cotb[1 - c].reshape(Z * 32, F), blend, NT, preferred_element_type=F32
            )
            igs[:, :, rs] = theirs.astype(BF16).reshape(Z, 32, tile)
            ours = lax.dot_general(cotb[c].reshape(Z * 32, F), blend, NT, preferred_element_type=F32)
            own[:, :, rs] = ours.reshape(Z, 32, tile)
            return carry

        lax.fori_loop(0, chunks[q] // tile, step, 0)
        cs = pl.ds(starts[q], chunks[q])
        chains[q]["core"] = send(
            igs.at[:, :, cs], igr.at[:, :, cs], ig_send.at[q, 0], ig_recv.at[q, 0], sibling
        )

    def ig_across(q):
        cs = pl.ds(starts[q], chunks[q])
        chains[q]["core"].wait_recv()
        rows = pl.ds(pl.multiple_of((1 - xh) * 16, 16), 16)
        for k in range(Z):
            xs[k, :, cs] = (own[k, rows, cs] + igr[k, rows, cs].astype(F32)).astype(BF16)
        chains[q]["x"] = send(
            xs.at[:, :, cs], xr.at[:, :, cs], ig_send.at[q, Z], ig_recv.at[q, Z], across
        )

    def ig_spread(q):
        cs = pl.ds(starts[q], chunks[q])
        chains[q]["x"].wait_recv()
        rows = pl.ds(pl.multiple_of(xh * 16, 16), 16)
        chains[q]["z"] = []
        for k in range(Z):
            to = (z + k) % Z
            total = own[to, rows, cs] + (igr[to, rows, cs].astype(F32) + xr[to, :, cs].astype(F32))
            if k == 0:
                acc[:, cs] = total
                continue
            zs[to, :, cs] = total.astype(BF16)
            chains[q]["z"].append(
                send(
                    zs.at[to, :, cs], zr.at[z, :, cs], ig_send.at[q, k], ig_recv.at[q, k],
                    (r, to * 4 + xh * 2 + c),
                )
            )

    def ig_end(q):
        cs = pl.ds(starts[q], chunks[q])
        for copy in chains[q]["z"]:
            copy.wait_recv()
        total = acc[:, cs]
        for k in range(1, Z):
            total = total + zr[(z + k) % Z, :, cs].astype(F32)
        input_out[:, cs] = total.astype(BF16)

    def out_dot(part_of, parts):
        span = F // parts

        def step(i, carry):
            cs = pl.ds(pl.multiple_of(part_of * span + i * tile, tile), tile)
            part = jnp.dot(
                tokb[...].reshape(2 * Z * 32, D), wv[:, cs], preferred_element_type=F32
            ).astype(BF16)
            part = part.reshape(2, Z, 32, tile)
            for a in range(2):
                ots[:, :, pl.ds(a * 32, 32), cs] = part[a].reshape(2, R // 2, 32, tile)
            return carry

        lax.fori_loop(0, span // tile, step, 0)

    side, place_y, ring_y = r // (R // 2), r % (R // 2), R // 2
    outs = [dict(), dict()]

    def out_send(h):
        cs = pl.ds(h * (F // 2), F // 2)
        outs[h]["y"] = []
        for k in range(1, ring_y):
            to = (place_y + k) % ring_y
            outs[h]["y"].append(
                send(
                    ots.at[:, to, :, cs], otr.at[:, place_y, :, cs], row_send.at[2 + h, k], row_recv.at[2 + h, k],
                    (side * ring_y + to, col),
                )
            )

    def out_turn(h):
        cs = pl.ds(h * (F // 2), F // 2)
        for copy in outs[h]["y"]:
            copy.wait_recv()

        def total(which):
            value = ots[which, place_y, :, cs].astype(F32)
            for k in range(1, ring_y):
                value = value + otr[which, (place_y + k) % ring_y, :, cs].astype(F32)
            return value

        oxs[:, cs] = total(1 - side).astype(BF16)
        outs[h]["x"] = send(
            oxs.at[:, cs], oxr.at[:, cs], row_send.at[2 + h, ring_y], row_recv.at[2 + h, ring_y],
            ((1 - side) * ring_y + place_y, col),
        )
        oacc[:, cs] = total(side)

    def out_end(h):
        cs = pl.ds(h * (F // 2), F // 2)
        outs[h]["x"].wait_recv()
        for a in range(2):
            for b in range(2):
                rows = pl.ds(a * 32 + b * 16, 16)
                value = oacc[rows, cs] + oxr[rows, cs].astype(F32)
                mixed_out[pl.ds((b * 2 + a) * 16, 16), cs] = value.astype(BF16)

    grads = []

    def grad_rows(t):
        rs = pl.ds(t * tile, tile)
        turned = tokb[:, :, :, rs].reshape(2 * Z * 32, tile).T

        for i in range(F // tile):
            cs = pl.ds(i * tile, tile)
            mg = jnp.dot(
                turned, cotb[:, :, :, cs].reshape(2 * Z * 32, tile), preferred_element_type=F32
            )
            wv[rs, cs] = (mg * slo[rs, cs]).astype(BF16)
            for b, pr in enumerate((pr0, pr1, pr2)):
                part = jnp.sum((mg * pr[rs, cs]).reshape(tile // 8, 8, tile), axis=0)
                sums[b, :, cs] = part if t == 0 else sums[b, :, cs] + part
        copy = pltpu.make_async_copy(wv.at[rs], wg_out.at[rs], wo_sem.at[t])
        copy.start()
        grads.append(copy)

    tiles = D // tile
    assert tiles == 8 and H == 4
    low, high = range(lanes // 2), range(lanes // 2, lanes)

    def blend(first, last, some=None):
        blend_rows(first * tile, last * tile, some)

    blend(0, 1)
    tok_step(0)
    blend(1, 3)
    tok_step(1)
    blend(3, 5)
    tok_step(2)
    for copy in cots:
        copy.wait_recv()
    ig_dot(0)
    blend(5, 6)
    tok_step(3)
    ig_across(0)
    blend(6, 8, low)
    for copy in sibs:
        copy.wait_recv()
    out_dot(0, 2)
    out_send(0)
    ig_dot(1)
    blend(6, 8, high)
    ig_across(1)
    ig_dot(2)
    out_dot(1, 2)
    ig_across(2)
    out_send(1)
    grad_rows(0)
    ig_spread(0)
    grad_rows(1)
    grad_rows(2)
    out_turn(0)
    grad_rows(3)
    grad_rows(4)
    ig_spread(1)
    for t in range(5, 8):
        grad_rows(t)
    for b in range(3):
        total = jnp.sum(sums[b], axis=0, keepdims=True)
        for i in range(lanes):
            trb[r, b, i : i + 1, :] = total[:, i * 128 : (i + 1) * 128]
    terms = [
        send(trb.at[r], trb.at[r], row_send.at[4, k], row_recv.at[4, k], ((r + k) % R, col)) for k in range(1, R)
    ]
    ig_spread(2)
    out_turn(1)
    out_end(0)
    ig_end(0)
    ig_end(1)
    for copy in terms:
        copy.wait_recv()
    total = trb[0]
    for i in range(1, R):
        total = total + trb[i]
    for i in range(lanes):
        cs = pl.ds(i * 128, 128)
        scaled = [coef[8 + b : 9 + b, cs] * total[b, i : i + 1, :] for b in range(3)]
        share = [coef[11 + b : 12 + b, cs] for b in range(3)]
        mean = share[0] * scaled[0] + share[1] * scaled[1] + share[2] * scaled[2]
        for b in range(3):
            lg_out[b : b + 1, cs] = share[b] * (mean - scaled[b])
    out_end(1)
    ig_end(2)
    for copy in sent:
        copy.wait_send()
    for copy in grads:
        copy.wait()


def place(cuts, *refs):
    sources, targets, held, come, gone = refs[:4], refs[4:8], refs[8:12], refs[12], refs[13]
    steps = []
    for n, src, dst, mid in zip(cuts, sources, targets, held):
        rows = src.shape[0] // n
        for k in range(n):
            cut = pl.ds(k * rows, rows)
            i = len(steps)
            steps.append(
                (
                    pltpu.make_async_copy(src.at[cut], mid.at[cut], come.at[i]),
                    pltpu.make_async_copy(mid.at[cut], dst.at[cut], gone.at[i]),
                )
            )
            steps[-1][0].start()
    for into, out in steps:
        into.wait()
        out.start()
    for _, out in steps:
        out.wait()


def shards(R, Z, tokens, weight, logits, cotangent):
    D, F = weight.shape
    H = Z // 2
    tile = D // 8
    chunks = (D // 2, D // 4, D // 4)
    T = 2 * Z * 32
    rows = cotangent.shape[0]
    n_w = 4
    vmem = pltpu.VMEM
    dma = pltpu.SemaphoreType.DMA
    scratch = [
        vmem((D, F), BF16), vmem((D, F), F32), vmem((D, F), F32), vmem((D, F), F32), vmem((D, F), F32),
        vmem((2, Z, 32, D), BF16), vmem((2, R, 32, F), BF16), vmem((16, F), F32),
        vmem((R, F // 128, 128), F32), vmem((R, 3, F // 128, 128), F32), vmem((3, 8, F), F32),
        vmem((Z, 32, D), BF16), vmem((Z, 32, D), BF16), vmem((Z, 32, D), F32),
        vmem((16, D), F32), vmem((Z, 16, D), BF16), vmem((Z, 16, D), BF16), vmem((Z, 16, D), BF16), vmem((Z, 16, D), BF16),
        vmem((2, R // 2, rows, F), BF16), vmem((2, R // 2, rows, F), BF16),
        vmem((rows, F), F32), vmem((rows, F), BF16), vmem((rows, F), BF16),
        dma((n_w,)), dma((5,)), dma((D // tile,)), dma((5, R)), dma((5, R)),
        dma((2 + 2 * H,)), dma((2 + 2 * H,)), dma((2, H)), dma((2, H)),
        dma((len(chunks), 2 + 2 * H)), dma((len(chunks), 2 + 2 * H)),
    ]
    results = pl.pallas_call(
        functools.partial(body, R, Z, chunks, tile),
        out_shape=(
            jax.ShapeDtypeStruct((rows, F), BF16),
            jax.ShapeDtypeStruct((16, D), BF16),
            jax.ShapeDtypeStruct((D, F), BF16),
            jax.ShapeDtypeStruct((3, F), F32),
        ),
        in_specs=[
            pl.BlockSpec(memory_space=pl.ANY), pl.BlockSpec(memory_space=pl.ANY),
            pl.BlockSpec(memory_space=vmem), pl.BlockSpec(memory_space=pl.ANY),
        ],
        out_specs=(
            pl.BlockSpec(memory_space=vmem), pl.BlockSpec(memory_space=vmem),
            pl.BlockSpec(memory_space=pl.ANY), pl.BlockSpec(memory_space=vmem),
        ),
        scratch_shapes=scratch,
        compiler_params=pltpu.CompilerParams(
            collective_id=0, has_side_effects=True, vmem_limit_bytes=59 * 2**20
        ),
    )(tokens, weight, logits, cotangent)
    cuts = (1, 1, 8, 1)
    return pl.pallas_call(
        functools.partial(place, cuts),
        out_shape=tuple(jax.ShapeDtypeStruct(v.shape, v.dtype) for v in results),
        in_specs=[pl.BlockSpec(memory_space=pl.ANY)] * 4,
        out_specs=[pl.BlockSpec(memory_space=pl.ANY)] * 4,
        scratch_shapes=[vmem(v.shape, v.dtype) for v in results] + [dma((sum(cuts),)), dma((sum(cuts),))],
    )(*results)


def solution(mesh):
    R, Z = mesh.shape["row"], mesh.shape["col"] // 4
    in_specs = (P("col", "row"), P("row", "col"), P(None, "col"), P("row", "col"))
    out_specs = (P("row", "col"), P("col", "row"), P("row", "col"), P(None, "col"))
    return jax.shard_map(
        functools.partial(shards, R, Z), mesh=mesh, in_specs=in_specs, out_specs=out_specs, check_vma=False
    )
```
